32 devices in a mesh: mem: 4 (over x, core), tile: 8 (over z, y).
Axes of the slice: x: 2, y: 2, z: 4, core: 2. Of those that a mesh axis runs over, the one named last changes fastest.
Arguments:
- latents: float32 [24, 256], P('mem'), may hold values from -6 to 6
- basis: bfloat16 [256, 2, 128, 512], P(None, None, 'tile'), may hold values from -0.375 to 0.375
- conv_in: bfloat16 [9, 64], replicated, may hold values from -2 to 2
- conv_mid: bfloat16 [9, 64, 64], replicated, may hold values from -0.25 to 0.25
- conv_out: bfloat16 [64], replicated, may hold values from -0.75 to 0.75
- pressure_prev: float32 [2, 128, 512], P(None, 'tile'), may hold values from -6 to 6
- source: float32 [2, 128, 512], P(None, 'tile'), may hold values from -6 to 6
- perf_cells: int32 [384, 8], replicated, may hold values from 0 to 131071
- perf_count: int32 [384], replicated, may hold values from 1 to 8
- obs_perturbed: float32 [24, 384], replicated, may hold values from -6 to 6
- obs_error: float32 [384], replicated, may hold values from 0.2 to 2
Outputs:
- pressure: float32 [24, 2, 128, 512], P(None, None, 'tile', 'mem')
- well_data: float32 [24, 384], replicated
- latents_new: float32 [24, 256], P('mem')
The draws below stay inside these ranges and needn't reach their ends.
All inputs are finite; a program needn't handle non-finite values.
Results may differ from the reference program's by a relative error of at most 0.0055.
Values may be sent and summed in bfloat16 or wider, within the bound.
No kernel may reach another device: no remote copies, remote signals or barrier semaphores. Data moves between devices by JAX's collectives and lax.ppermute only.
A program may use at most 128 MiB of HBM per device.

```python
import math
import jax
import jax.numpy as jnp
from jax import lax

NZ = 2
L = 256
C = 64
WELLS = 384
PERF = 8
SWEEPS = 2
MEMBERS = 24
NX = 128
NY = 512


def with_ends(array, stream_key, least, largest):
    shape = array.shape
    place = [jax.random.randint(jax.random.fold_in(stream_key, axis), (), 0, shape[axis]) for axis in range(len(shape))]
    array = array.at[tuple(place)].set(least)
    longest = shape.index(max(shape))
    place[longest] = (place[longest] + 1) % shape[longest]
    return array.at[tuple(place)].set(largest)


def level_of(key, extent, shards, smallest, top_value):
    level, own = 1.0, jax.random.fold_in(key, 6)
    for dim, shards_of in shards:
        draws = jnp.exp(jax.random.uniform(jax.random.fold_in(own, dim), (shards_of,), jnp.float32, smallest / len(shards), top_value / len(shards)))
        level = level * jnp.repeat(draws, extent[dim] // shards_of).reshape([-1 if axis == dim else 1 for axis in range(len(extent))])
    return level


def noise(stream_key, dims, scale, limit, cuts=(), held_as=jnp.bfloat16):
    result = jax.random.normal(stream_key, dims, jnp.float32) * scale
    if len(cuts) > 0:
        result = level_of(stream_key, dims, cuts, -0.22, 0.18) * result
    return jnp.clip(result, min=-limit, max=limit).astype(held_as)


def setup_inputs(seed: int = 0) -> dict:
    streams_of = jax.random.split(jax.random.key(seed), 12)
    latents = noise(streams_of[0], (MEMBERS, L), 1.0, 6.0, ((0, 4),), jnp.float32)
    basis = noise(streams_of[1], (L, NZ, NX, NY), L ** -0.5, 0.375, ((2, 8),))
    conv_in = noise(streams_of[2], (9, C), 9 ** -0.5, 2.0)
    conv_mid = noise(streams_of[3], (9, C, C), (9 * C) ** -0.5, 0.25)
    conv_out = noise(streams_of[4], (C,), C ** -0.5, 0.75)
    pressure_prev = noise(streams_of[5], (NZ, NX, NY), 1.0, 6.0, ((1, 8),), jnp.float32)
    source = noise(streams_of[6], (NZ, NX, NY), 1.0, 6.0, ((1, 8),), jnp.float32)
    perf_cells = with_ends(jax.random.randint(streams_of[7], (WELLS, PERF), 0, NZ * NX * NY), jax.random.fold_in(streams_of[7], 1), 0, (NZ * NX * NY) - 1).astype(jnp.int32)
    perf_count = with_ends(jax.random.randint(streams_of[8], (WELLS,), 1, PERF + 1), jax.random.fold_in(streams_of[8], 1), 1, PERF).astype(jnp.int32)
    obs_perturbed = noise(streams_of[9], (MEMBERS, WELLS), 1.0, 6.0, (), jnp.float32)
    obs_error = jnp.clip(jnp.exp(jax.random.uniform(streams_of[10], (WELLS,), jnp.float32, math.log(0.2), math.log(2.0))), 0.2, 2.0)
    return dict(latents=latents, basis=basis, conv_in=conv_in, conv_mid=conv_mid, conv_out=conv_out, pressure_prev=pressure_prev, source=source, perf_cells=perf_cells, perf_count=perf_count, obs_perturbed=obs_perturbed, obs_error=obs_error)


storage_coef = 1.0

def lift(field, conv_in):
    rows = field.shape[1] - 2
    width = field.shape[2]
    padded = jnp.pad(field, ((0, 0), (0, 0), (1, 1)))
    total = jnp.zeros((field.shape[0], conv_in.shape[1], rows, width), jnp.float32)
    for tap in range(9):
        part = padded[:, tap // 3:tap // 3 + rows, tap % 3:tap % 3 + width]
        total = total + conv_in[tap].astype(jnp.float32)[None, :, None, None] * part[:, None]
    return jax.nn.relu(total).astype(jnp.bfloat16)

def mix(lifted, field, conv_mid, conv_out):
    rows = field.shape[1]
    width = field.shape[2]
    padded = jnp.pad(lifted.astype(jnp.float32), ((0, 0), (0, 0), (0, 0), (1, 1)))
    total = jnp.zeros((field.shape[0], conv_mid.shape[1], rows, width), jnp.float32)
    for tap in range(9):
        part = padded[:, :, tap // 3:tap // 3 + rows, tap % 3:tap % 3 + width]
        total = total + jnp.einsum('oc,zcxy->zoxy', conv_mid[tap].astype(jnp.float32), part)
    deep = jax.nn.relu(total)
    return field + jnp.einsum('c,zcxy->zxy', conv_out.astype(jnp.float32), deep)

def neighbours(wide):
    zpad = jnp.pad(wide, ((0, 0), (1, 1), (0, 0), (0, 0)))
    return [zpad[:, 1:-1, 2:, 1:-1], zpad[:, 1:-1, :-2, 1:-1], zpad[:, 1:-1, 1:-1, 2:], zpad[:, 1:-1, 1:-1, :-2], zpad[:, 2:, 1:-1, 1:-1], zpad[:, :-2, 1:-1, 1:-1]]

def widen(values):
    return jnp.pad(values, ((0, 0), (0, 0), (1, 1), (1, 1)))

def reference(latents, basis, conv_in, conv_mid, conv_out, pressure_prev, source, perf_cells, perf_count, obs_perturbed, obs_error):
    flat_basis = basis.reshape(basis.shape[0], -1)
    field = jnp.dot(latents.astype(jnp.bfloat16).astype(jnp.float32), flat_basis.astype(jnp.float32), preferred_element_type=jnp.float32)
    field = field.reshape(MEMBERS, NZ, NX, NY)

    def decode(single):
        wide = jnp.pad(single, ((0, 0), (1, 1), (0, 0)))
        lifted = lift(wide, conv_in)
        lifted_wide = jnp.pad(lifted, ((0, 0), (0, 0), (1, 1), (0, 0)))
        return mix(lifted_wide, single, conv_mid, conv_out)
    log_perm = lax.map(decode, field)
    perm = jnp.exp(log_perm)
    conduct = [2.0 * perm * other / (perm + other) for other in neighbours(widen(perm))]
    denom = storage_coef + sum(conduct)
    base = storage_coef * pressure_prev + source
    press = jnp.broadcast_to(pressure_prev, perm.shape).astype(jnp.float32)
    for sweep in range(SWEEPS):
        near = neighbours(widen(press))
        acc = base[None] + sum((cval * nval for cval, nval in zip(conduct, near)))
        press = acc / denom
    ids = perf_cells.reshape(-1).astype(jnp.int32)
    perm_at = jnp.take(perm.reshape(MEMBERS, -1), ids, axis=1).reshape(MEMBERS, WELLS, PERF)
    press_at = jnp.take(press.reshape(MEMBERS, -1), ids, axis=1).reshape(MEMBERS, WELLS, PERF)
    used = (jnp.arange(PERF)[None, :] < perf_count[:, None]).astype(jnp.float32)
    numer = lax.optimization_barrier(jnp.sum(perm_at * press_at * used[None], axis=2))
    weight_sum = lax.optimization_barrier(jnp.sum(perm_at * used[None], axis=2))
    well_data = numer / weight_sum
    scale = 2.0 * obs_error
    centred = well_data - lax.optimization_barrier(jnp.mean(well_data, axis=0, keepdims=True))
    scaled = centred / (math.sqrt(MEMBERS - 1) * scale[None, :])
    innov = (obs_perturbed - well_data) / scale[None, :]
    gram = jnp.eye(MEMBERS, dtype=jnp.float32) + jnp.dot(scaled, scaled.T, precision=lax.Precision.HIGHEST)
    cross = jnp.dot(scaled, innov.T, precision=lax.Precision.HIGHEST)
    factor = jnp.linalg.cholesky(gram)
    weights = jax.scipy.linalg.cho_solve((factor, True), cross)
    spread = (latents - lax.optimization_barrier(jnp.mean(latents, axis=0, keepdims=True))) / math.sqrt(MEMBERS - 1)
    latents_new = latents + jnp.dot(weights.T, spread, precision=lax.Precision.HIGHEST)
    return (press, well_data, latents_new)
```

```python
import functools
import math

import jax
import jax.numpy as jnp
from jax import lax
from jax.experimental import pallas as pl
from jax.experimental.pallas import tpu as pltpu
from jax.sharding import PartitionSpec as P

SWEEPS = 2
HALO = 4
RING = 24
LIFT_BLOCKS = 11
MIX_BLOCKS = 10
SEG = 16
BF = jnp.bfloat16
F32 = jnp.float32
VMEM = pl.BlockSpec(memory_space=pltpu.VMEM)
SMEM = pl.BlockSpec(memory_space=pltpu.SMEM)


def iota(shape, dim):
    return lax.broadcasted_iota(jnp.int32, shape, dim)


def field_kernel(lat_ref, basis_ref, prev_ref, src_ref, field_ref, low_ref, high_ref):
    step = pl.program_id(0)
    comps, layers, rows, width = basis_ref.shape
    members, total = lat_ref.shape
    span = comps * rows

    @pl.when(step == 0)
    def _():
        field_ref[...] = jnp.zeros_like(field_ref)

    pick = (iota((total, span), 0) == step * comps + iota((total, span), 1) // rows).astype(BF)
    spread = jnp.dot(lat_ref[...].astype(BF), pick, preferred_element_type=F32)
    own = iota((rows, span), 0) == iota((rows, span), 1) % rows
    left = jnp.where(own[None], spread[:, None, :], 0.0).astype(BF).reshape(members * rows, span)
    for z in range(layers):
        right = basis_ref[:, z].reshape(span, width)
        part = jnp.dot(left, right, preferred_element_type=F32)
        field_ref[z] = field_ref[z] + part.reshape(members, rows, width)

    @pl.when(step == pl.num_programs(0) - 1)
    def _():
        tiles = [field_ref.at[z, m] for z in range(layers) for m in range(members)]
        tiles += [prev_ref.at[z] for z in range(layers)] + [src_ref.at[z] for z in range(layers)]
        first = iota((8, width), 0) < HALO
        for pair in range(len(tiles) // 2):
            even, odd = tiles[2 * pair], tiles[2 * pair + 1]
            low_ref[pair] = jnp.where(first, even[0:8], pltpu.roll(odd[0:8], HALO, 0))
            high_ref[pair] = jnp.where(first, pltpu.roll(odd[rows - 8 : rows], HALO, 0), even[rows - 8 : rows])


def field_of(latents, basis, prev, src):
    total, layers, rows, width = basis.shape
    members = latents.shape[0]
    comps = 32
    pairs = (layers * members + 2 * layers) // 2
    whole = lambda shape: pl.BlockSpec(shape, lambda s: (0,) * len(shape))
    return pl.pallas_call(
        field_kernel,
        grid=(total // comps,),
        in_specs=[
            whole(latents.shape),
            pl.BlockSpec((comps, layers, rows, width), lambda s: (s, 0, 0, 0)),
            whole(prev.shape),
            whole(src.shape),
        ],
        out_specs=[
            whole((layers, members, rows, width)),
            whole((pairs, 8, width)),
            whole((pairs, 8, width)),
        ],
        out_shape=[
            jax.ShapeDtypeStruct((layers, members, rows, width), F32),
            jax.ShapeDtypeStruct((pairs, 8, width), F32),
            jax.ShapeDtypeStruct((pairs, 8, width), F32),
        ],
        compiler_params=pltpu.CompilerParams(vmem_limit_bytes=24 * 2**20),
    )(latents, basis, prev, src)


def block_row(block, half):
    return jnp.where(block == 0, jnp.where(half == 0, 18, -3), 2 * block - HALO + half)


def prep_kernel(grid_rows, rows, tile_ref, taps_ref, mid_ref, win_ref, wmix_ref):
    tile = tile_ref[0]
    shape = taps_ref.shape
    kinds = jnp.where(iota(shape, 0) >> 4 == iota(shape, 1) >> 6, taps_ref[...].astype(F32), 0.0).astype(BF)
    k, j = iota((256, 64), 0), iota((256, 64), 1)
    offset, ring = k >> 6, k & 31
    place, tap = j >> 4, j & 15
    xx, yy = place >> 1, place & 1
    a = ((tap * 11) >> 5) - 1
    b = tap - 3 * (a + 1) - 1
    fits = (tap < 9) & (offset == yy + b + 1)
    for block in range(LIFT_BLOCKS):
        if block == 0:
            row = jnp.where(xx == 0, 18, -3)
        else:
            row = 2 * block - HALO + xx
        near = row + a
        near = jnp.where(near < 0, near + RING, near)
        grid_row = tile * rows + row
        pick = fits & (ring == near) & (grid_row >= 0) & (grid_row < grid_rows)
        win_ref[block] = jnp.dot(jnp.where(pick, 1.0, 0.0).astype(BF), kinds, preferred_element_type=F32).astype(BF)
    o, n = iota((64, 256), 0), iota((64, 256), 1)
    placed = []
    for place_out in range(4):
        put = n == (o >> 5) * 128 + place_out * 32 + (o & 31)
        placed.append(jnp.dot(mid_ref[...], jnp.where(put, 1.0, 0.0).astype(BF), preferred_element_type=F32))
    for kind in range(4):
        side, over = kind & 1, kind >> 1
        for place_in in range(4):
            xi, yi = place_in >> 1, place_in & 1
            total = jnp.zeros((64, 256), F32)
            for place_out in range(4):
                xo, yo = place_out >> 1, place_out & 1
                dx = xi - xo + (0 if not over else (2 if xi == 0 else -2))
                dy = yi - yo + (0 if not side else (2 if yi == 0 else -2))
                if abs(dx) <= 1 and abs(dy) <= 1:
                    t = 3 * (dx + 1) + dy + 1
                    total = total + placed[place_out][64 * t : 64 * t + 64]
            at = 256 * kind + 64 * place_in
            wmix_ref[at : at + 64, :] = total.astype(BF)


def prep(tile_at, grid_rows, rows, conv_in, conv_mid):
    taps = jnp.tile(jnp.pad(conv_in, ((0, 7), (0, 0))), (4, 4))
    mid = jnp.transpose(conv_mid, (0, 2, 1)).reshape(-1, conv_mid.shape[1])
    return pl.pallas_call(
        functools.partial(prep_kernel, grid_rows, rows),
        in_specs=[SMEM, VMEM, VMEM],
        out_specs=[VMEM, VMEM],
        out_shape=[
            jax.ShapeDtypeStruct((LIFT_BLOCKS, 256, 256), BF),
            jax.ShapeDtypeStruct((1024, 256), BF),
        ],
        compiler_params=pltpu.CompilerParams(vmem_limit_bytes=24 * 2**20),
        cost_estimate=pl.CostEstimate(flops=400_000_000, bytes_accessed=4_000_000, transcendentals=0),
    )(tile_at, taps, mid)


def ring_tile(group, up_ref, down_ref):
    pair = group // 2
    up, down = up_ref[pair], down_ref[pair]
    first = iota(up.shape, 0) < HALO
    return jnp.where(first, up, down), pltpu.roll(jnp.where(first, down, up), HALO, 0)


def decode_kernel(
    grid_rows,
    tile_ref,
    field_ref,
    down_ref,
    up_ref,
    prev_ref,
    src_ref,
    win_ref,
    wmix_ref,
    out_ref,
    sel_ref,
    col_ref,
    press_ref,
    sums_ref,
    f_scr,
    t_scr,
    pt_scr,
    lift_scr,
    side_scr,
    deep_scr,
    wout_scr,
    v_scr,
):
    layers, members, rows, width = field_ref.shape
    groups = layers * members
    steps = width // (2 * SEG)
    block_rows = width // 2
    tile = tile_ref[0]

    def load(pair, _):
        up, down = up_ref[pair], down_ref[pair]
        first = iota(up.shape, 0) < HALO
        thirds = (jnp.where(first, up, down), pltpu.roll(jnp.where(first, down, up), HALO, 0))
        for half in range(2):
            group = 2 * pair + half
            own = field_ref[group // members, lax.rem(group, members)]
            f = jnp.concatenate([own, thirds[half]], axis=0)
            f_scr[group] = f
            hi = f.astype(BF).astype(F32)
            lo = f - hi
            zero = jnp.zeros((32 - RING, width), F32)
            edge = iota((RING, width), 1) == 0
            hi_left = jnp.where(edge, 0.0, pltpu.roll(hi, 1, 1))
            lo_left = jnp.where(edge, 0.0, pltpu.roll(lo, 1, 1))
            tall = jnp.concatenate([hi_left, zero, lo_left, zero, hi, zero, lo, zero], axis=0).T
            t_scr[0:width, :] = tall
            end = pltpu.roll(tall[width - 8 : width], 64, 1)
            end = jnp.where(iota(end.shape, 1) < 64, end, 0.0)
            t_scr[width : width + 8, :] = pltpu.roll(end, 1, 0)
            for q in range(steps + 1):
                part = t_scr[pl.ds(2 * q, SEG, stride=2 * steps), :].astype(BF)
                if q < steps:
                    pt_scr[pl.ds(pl.multiple_of(group * block_rows + q * SEG, SEG), SEG), 0:128] = part
                if q > 0:
                    pt_scr[pl.ds(pl.multiple_of(group * block_rows + (q - 1) * SEG, SEG), SEG), 128:256] = part
        return 0

    lax.fori_loop(0, groups // 2, load, 0)

    chunk = 4 * block_rows
    chunks = groups * block_rows // chunk

    def lift(t, _):
        block, part = t // chunks, lax.rem(t, chunks)
        at = pl.multiple_of(part * chunk, chunk)
        wide = jnp.dot(pt_scr[pl.ds(at, chunk), :], win_ref[block], preferred_element_type=F32)
        wide = jnp.maximum(wide, 0.0)
        tight = wide.astype(BF)
        lift_scr[block, pl.ds(at, chunk), :] = tight
        right = iota((SEG, 256), 1) & 64 == 0
        row = iota((SEG, 256), 0)
        for i in range(chunk // block_rows):
            base = i * block_rows
            last = base + block_rows - SEG
            after = jnp.where(row < SEG - 1, pltpu.roll(wide[base : base + SEG], SEG - 1, 0), 0.0)
            before = jnp.where(row > 0, pltpu.roll(wide[last : last + SEG], 1, 0), 0.0)
            for q in range(steps):
                r = base + q * SEG
                nxt = after if q == steps - 1 else wide[r + SEG : r + 2 * SEG]
                prv = before if q == 0 else wide[r - SEG : r]
                side_scr[block, pl.ds(pl.multiple_of(at + r, SEG), SEG), :] = jnp.where(right, nxt, prv).astype(BF)
        return 0

    lax.fori_loop(0, LIFT_BLOCKS * chunks, lift, 0)

    gain0, gain1 = out_ref[0:1, :], out_ref[1:2, :]

    def mix(t, _):
        block, part = t // chunks + 1, lax.rem(t, chunks)
        above = block - 1
        below = jnp.where(block == LIFT_BLOCKS - 1, 0, block + 1)
        at = pl.ds(pl.multiple_of(part * chunk, chunk), chunk)
        x = jnp.concatenate(
            [
                lift_scr[block, at, :],
                side_scr[block, at, :],
                lift_scr[below, at, 0:128],
                lift_scr[above, at, 128:256],
                side_scr[below, at, 0:128],
                side_scr[above, at, 128:256],
            ],
            axis=1,
        )
        deep = jnp.maximum(jnp.dot(x, wmix_ref[...], preferred_element_type=F32), 0.0)
        deep_scr[block - 1, at, :] = (deep[:, :128] * gain0 + deep[:, 128:] * gain1).astype(BF)
        return 0

    lax.fori_loop(0, MIX_BLOCKS * chunks, mix, 0)

    k, n = iota(wout_scr.shape, 0), iota(wout_scr.shape, 1)
    place = (k & 127) >> 5
    row = 2 * ((k >> 7) + 1) - HALO + (place >> 1)
    row = jnp.where(row < 0, row + RING, row)
    wout_scr[...] = jnp.where(n == (place & 1) * 32 + row, 1.0, 0.0).astype(BF)

    def collect(pair, _):
        at = pl.ds(pl.multiple_of(pair * 2 * block_rows, 2 * block_rows), 2 * block_rows)
        x = jnp.concatenate([deep_scr[j, at, :] for j in range(MIX_BLOCKS)], axis=1)
        both = jnp.dot(x, wout_scr[...], preferred_element_type=F32)
        both = both[:block_rows] + pltpu.roll(both[block_rows:], 64, 1)
        for q in range(steps):
            part = both[q * SEG : (q + 1) * SEG]
            t_scr[pl.ds(2 * q, SEG, stride=2 * steps), :] = part
            t_scr[pl.ds(2 * q + 1, SEG, stride=2 * steps), :] = part
        flat = t_scr[0:width, :].T
        even = iota((RING, width), 1) & 1 == 0
        for half in range(2):
            s = 64 * half
            f_scr[2 * pair + half] = f_scr[2 * pair + half] + jnp.where(
                even, flat[s : s + RING], flat[s + 32 : s + 32 + RING]
            )
        return 0

    lax.fori_loop(0, groups // 2, collect, 0)

    full = (RING, width)
    ring = iota(full, 0)
    grid_row = tile * rows + jnp.where(ring < rows + HALO, ring, ring - RING)
    inside = (grid_row >= 0) & (grid_row < grid_rows)
    joined = (grid_row >= 0) & (grid_row < grid_rows - 1)
    not_last = iota(full, 1) < width - 1

    def ring_of(ref, group, z):
        pair = group // 2
        up, down = up_ref[pair], down_ref[pair]
        first = iota(up.shape, 0) < HALO
        if group % 2 == 0:
            third = jnp.where(first, up, down)
        else:
            third = pltpu.roll(jnp.where(first, down, up), HALO, 0)
        return jnp.concatenate([ref[z], third], axis=0)

    def row_next(v):
        return pltpu.roll(v, RING - 1, 0)

    def row_prev(v):
        return pltpu.roll(v, 1, 0)

    def col_next(v):
        return pltpu.roll(v, width - 1, 1)

    def col_prev(v):
        return pltpu.roll(v, 1, 1)

    start = [ring_of(prev_ref, groups + z, z) for z in range(layers)]
    base = [start[z] + ring_of(src_ref, groups + layers + z, z) for z in range(layers)]
    around = [[f(start[z]) for f in (row_next, row_prev, col_next, col_prev)] for z in range(layers)]

    def flow(p, q):
        return 2.0 * p * q / (p + q)

    def sweep(member, _):
        perm = [jnp.where(inside, jnp.exp(f_scr[z * members + member]), 1.0) for z in range(layers)]
        between = jnp.where(inside, flow(perm[0], perm[1]), 0.0)
        faces, scale = [], []
        for z in range(layers):
            below = jnp.where(joined, flow(perm[z], row_next(perm[z])), 0.0)
            right = jnp.where(not_last, flow(perm[z], col_next(perm[z])), 0.0)
            right = jnp.where(inside, right, 0.0)
            face = (below, row_prev(below), right, col_prev(right))
            faces.append(face)
            scale.append(1.0 / (1.0 + between + face[0] + face[1] + face[2] + face[3]))
        press, near = start, around
        for turn in range(SWEEPS):
            if turn > 0:
                near = [[f(press[z]) for f in (row_next, row_prev, col_next, col_prev)] for z in range(layers)]
            press = [
                (base[z] + between * press[1 - z] + sum(c * v for c, v in zip(faces[z], near[z]))) * scale[z]
                for z in range(layers)
            ]
        cols = press_ref.shape[4]
        for z in range(layers):
            for d in range(press_ref.shape[0]):
                press_ref[d, member, z] = press[z][:rows, d * cols : (d + 1) * cols]
            weight = perm[z][:rows]
            for kind, value in enumerate((weight * press[z][:rows], weight)):
                hi = value.astype(BF)
                lo = (value - hi.astype(F32)).astype(BF)
                for part, piece in enumerate((hi, lo)):
                    at = (((kind * 2 + part) * members + member) * layers + z) * rows
                    v_scr[pl.ds(pl.multiple_of(at, rows), rows), :] = piece
        return 0

    lax.fori_loop(0, members, sweep, 0)

    slots, wells = sel_ref.shape
    cells = layers * rows
    sums = jnp.zeros((4 * members, wells), F32)
    for slot in range(slots):
        here = iota((width, wells), 0) == col_ref[slot : slot + 1, :]
        got = jnp.dot(v_scr[...], jnp.where(here, 1.0, 0.0).astype(BF), preferred_element_type=F32)
        mine = iota((cells, wells), 0) == sel_ref[slot : slot + 1, :]
        picked = jnp.where(mine[None], got.reshape(4 * members, cells, wells), 0.0)
        sums = sums + jnp.sum(picked, axis=1)
    sums_ref[0:members] = sums[0:members] + sums[members : 2 * members]
    sums_ref[members : 2 * members] = sums[2 * members : 3 * members] + sums[3 * members :]


def decode(parts, tile_at, grid_rows, field, down, up, prev, src, win, wmix, gains, sel, col):
    layers, members, rows, width = field.shape
    groups = layers * members
    total = groups * width // 2
    wells = sel.shape[1]
    return pl.pallas_call(
        functools.partial(decode_kernel, grid_rows),
        in_specs=[SMEM] + [VMEM] * 10,
        out_specs=[VMEM, VMEM],
        out_shape=[
            jax.ShapeDtypeStruct((parts, members, layers, rows, width // parts), F32),
            jax.ShapeDtypeStruct((2 * members, wells), F32),
        ],
        scratch_shapes=[
            pltpu.VMEM((groups, RING, width), F32),
            pltpu.VMEM((width + 8, 128), F32),
            pltpu.VMEM((total, 256), BF),
            pltpu.VMEM((LIFT_BLOCKS, total, 256), BF),
            pltpu.VMEM((LIFT_BLOCKS, total, 256), BF),
            pltpu.VMEM((MIX_BLOCKS, total, 128), BF),
            pltpu.VMEM((MIX_BLOCKS * 128, 128), BF),
            pltpu.VMEM((4 * groups * rows, width), BF),
        ],
        compiler_params=pltpu.CompilerParams(vmem_limit_bytes=60 * 2**20),
    )(tile_at, field, down, up, prev, src, win, wmix, gains, sel, col)


def update_kernel(mem_ref, wd_refs, lat_refs, obs_ref, err_ref, data_ref, new_ref, wd_scr, lat_scr, step_scr):
    count = len(wd_refs)
    own, wells = wd_refs[0].shape
    members = count * own
    mem = mem_ref[0]
    for k in range(count):
        source = lax.rem(mem + count - k, count)
        wd_scr[source] = wd_refs[k][...]
        lat_scr[source] = lat_refs[k][...]
    data = jnp.concatenate([wd_scr[k] for k in range(count)], axis=0)
    every = jnp.concatenate([lat_scr[k] for k in range(count)], axis=0)
    data_ref[...] = data
    scale = 2.0 * err_ref[...]
    root = math.sqrt(members - 1)
    scaled = (data - jnp.mean(data, axis=0, keepdims=True)) / (root * scale)
    innov = (obs_ref[...] - data) / scale
    dims = (((1,), (1,)), ((), ()))
    exact = lax.Precision.HIGHEST
    eye = (iota((members, members), 0) == iota((members, members), 1)).astype(F32)
    gram = eye + lax.dot_general(scaled, scaled, dims, precision=exact, preferred_element_type=F32)
    cross = lax.dot_general(innov, scaled, dims, precision=exact, preferred_element_type=F32)
    right = (every - jnp.mean(every, axis=0, keepdims=True)) / root
    place = iota((members, 1), 0)
    for k in range(members):
        inverse = 1.0 / gram[k : k + 1, k : k + 1]
        factor = jnp.where(place == k, 0.0, gram[:, k : k + 1])
        gram_row = gram[k : k + 1, :] * inverse
        right_row = right[k : k + 1, :] * inverse
        gram = jnp.where(place == k, gram_row, gram - factor * gram_row)
        right = jnp.where(place == k, right_row, right - factor * right_row)
    new = every + jnp.dot(cross, right, precision=exact, preferred_element_type=F32)
    for k in range(count):
        step_scr[k] = new[k * own : (k + 1) * own]
    new_ref[...] = step_scr[mem]


def update(mem_at, wds, lats, obs, err):
    count = len(wds)
    own, wells = wds[0].shape
    width = lats[0].shape[1]

    def kernel(mem_ref, *refs):
        update_kernel(mem_ref, refs[:count], refs[count : 2 * count], *refs[2 * count :])

    return pl.pallas_call(
        kernel,
        in_specs=[SMEM] + [VMEM] * (2 * count + 2),
        out_specs=[VMEM, VMEM],
        out_shape=[
            jax.ShapeDtypeStruct((count * own, wells), F32),
            jax.ShapeDtypeStruct((own, width), F32),
        ],
        scratch_shapes=[
            pltpu.VMEM((count, own, wells), F32),
            pltpu.VMEM((count, own, width), F32),
            pltpu.VMEM((count, own, width), F32),
        ],
        compiler_params=pltpu.CompilerParams(vmem_limit_bytes=24 * 2**20),
    )(mem_at, *wds, *lats, obs, err)


def gathered(own, axis):
    count = lax.axis_size(axis)
    return [own] + [
        lax.ppermute(own, axis, [(i, (i + k) % count) for i in range(count)]) for k in range(1, count)
    ]


def summed(own, axis):
    count = lax.axis_size(axis)
    if count & (count - 1):
        return lax.psum(own, axis)
    k = 1
    while k < count:
        own = own + lax.ppermute(own, axis, [(i, i ^ k) for i in range(count)])
        k *= 2
    return own


def body(
    latents,
    basis,
    conv_in,
    conv_mid,
    conv_out,
    pressure_prev,
    source,
    perf_cells,
    perf_count,
    obs_perturbed,
    obs_error,
):
    members = latents.shape[0]
    layers, rows, width = basis.shape[1:]
    tiles = lax.axis_size("tile")
    parts = lax.axis_size("mem")
    grid_rows = rows * tiles
    tile_at = lax.axis_index("tile")
    tile_vec = tile_at.astype(jnp.int32).reshape(1)
    mem_vec = lax.axis_index("mem").astype(jnp.int32).reshape(1)

    field, low, high = field_of(latents, basis, pressure_prev, source)
    down = lax.ppermute(high, "tile", [(i, i + 1) for i in range(tiles - 1)])
    up = lax.ppermute(low, "tile", [(i + 1, i) for i in range(tiles - 1)])
    lats = gathered(latents, "mem")

    win, wmix = prep(tile_vec, grid_rows, rows, conv_in, conv_mid)
    gains = jnp.tile(conv_out.astype(F32).reshape(2, 32), (1, 4))
    ids = perf_cells.T
    slots = ids.shape[0]
    layer_at = ids // (grid_rows * width)
    rest = ids % (grid_rows * width)
    row_at = rest // width - tile_at * rows
    used = (jnp.arange(slots)[:, None] < perf_count[None, :]) & (row_at >= 0) & (row_at < rows)
    sel = jnp.where(used, layer_at * rows + row_at, -1)
    col = rest % width

    press, sums = decode(
        parts, tile_vec, grid_rows, field, down, up, pressure_prev, source, win, wmix, gains, sel, col
    )
    swapped = lax.all_to_all(press, "mem", 0, 0)
    sums = summed(sums, "tile")
    wds = gathered(sums[:members] / sums[members:], "mem")
    data, new = update(mem_vec, wds, lats, obs_perturbed, obs_error.reshape(1, -1))
    return (swapped.reshape((parts * members,) + swapped.shape[2:]), data, new)


def solution(mesh):
    return jax.shard_map(
        body,
        mesh=mesh,
        in_specs=(
            P("mem", None),
            P(None, None, "tile", None),
            P(),
            P(),
            P(),
            P(None, "tile", None),
            P(None, "tile", None),
            P(),
            P(),
            P(),
            P(),
        ),
        out_specs=(P(None, None, "tile", "mem"), P(), P("mem", None)),
        check_vma=False,
    )
```

```python
import functools
import math

import jax
import jax.numpy as jnp
from jax import lax
from jax.experimental import pallas as pl
from jax.experimental.pallas import tpu as pltpu
from jax.sharding import PartitionSpec as P

SWEEPS = 2
HALO = 4
RING = 24
LIFT_BLOCKS = 11
MIX_BLOCKS = 10
CHUNK_GROUPS = 12
SEG = 16
BF = jnp.bfloat16
F32 = jnp.float32
VMEM = pl.BlockSpec(memory_space=pltpu.VMEM)
SMEM = pl.BlockSpec(memory_space=pltpu.SMEM)


def iota(shape, dim):
    return lax.broadcasted_iota(jnp.int32, shape, dim)


def place_weights(tile, grid_rows, rows, in_ref, mid_ref, out_ref, win_ref, wmix_ref, gain_ref):
    one = lambda mask: jnp.where(mask, 1.0, 0.0).astype(BF)
    dot = functools.partial(jnp.dot, preferred_element_type=F32)
    taps = dot(one(iota((64, 9), 0) & 15 == iota((64, 9), 1)), in_ref[...]).astype(BF)
    taps = dot(taps, one(iota((64, 256), 0) == iota((64, 256), 1) & 63))
    kinds = jnp.where(iota((64, 256), 0) >> 4 == iota((64, 256), 1) >> 6, taps, 0.0).astype(BF)
    k, j = iota((256, 64), 0), iota((256, 64), 1)
    offset, ring = k >> 6, k & 31
    place, tap = j >> 4, j & 15
    xx, yy = place >> 1, place & 1
    a = ((tap * 11) >> 5) - 1
    b = tap - 3 * (a + 1) - 1
    fits = (tap < 9) & (offset == yy + b + 1)
    for block in range(LIFT_BLOCKS):
        row = jnp.where(xx == 0, 18, -3) if block == 0 else 2 * block - HALO + xx
        near = row + a
        near = jnp.where(near < 0, near + RING, near)
        grid_row = tile * rows + row
        pick = fits & (ring == near) & (grid_row >= 0) & (grid_row < grid_rows)
        win_ref[block] = dot(one(pick), kinds).astype(BF)
    o, n = iota((64, 1024), 0), iota((64, 1024), 1)
    put = one(n & 255 == (o >> 5) * 128 + (n >> 8) * 32 + (o & 31))
    placed = [
        lax.dot_general(mid_ref[t], put, (((0,), (0,)), ((), ())), preferred_element_type=F32) for t in range(9)
    ]
    for kind in range(4):
        side, over = kind & 1, kind >> 1
        for place_in in range(4):
            xi, yi = place_in >> 1, place_in & 1
            total = jnp.zeros((64, 256), F32)
            for place_out in range(4):
                xo, yo = place_out >> 1, place_out & 1
                dx = xi - xo + (0 if not over else (2 if xi == 0 else -2))
                dy = yi - yo + (0 if not side else (2 if yi == 0 else -2))
                if abs(dx) <= 1 and abs(dy) <= 1:
                    t = 3 * (dx + 1) + dy + 1
                    total = total + placed[t][:, 256 * place_out : 256 * place_out + 256]
            at = 256 * kind + 64 * place_in
            wmix_ref[at : at + 64, :] = total.astype(BF)
    gains = jnp.broadcast_to(out_ref[...].astype(F32), (8, 64)).astype(BF)
    c, n = iota((64, 128), 0), iota((64, 128), 1)
    gain_ref[0:8] = dot(gains, one(c == n & 31))
    gain_ref[8:16] = dot(gains, one(c == 32 + (n & 31)))


def place_kernel(grid_rows, rows, tile_ref, in_ref, mid_ref, out_ref, win_ref, wmix_ref, gain_ref):
    place_weights(tile_ref[0], grid_rows, rows, in_ref, mid_ref, out_ref, win_ref, wmix_ref, gain_ref)


def placed(tile_vec, grid_rows, rows, conv_in, conv_mid, conv_out):
    return pl.pallas_call(
        functools.partial(place_kernel, grid_rows, rows),
        in_specs=[SMEM] + [VMEM] * 3,
        out_specs=[VMEM] * 3,
        out_shape=[
            jax.ShapeDtypeStruct((LIFT_BLOCKS, 256, 256), BF),
            jax.ShapeDtypeStruct((1024, 256), BF),
            jax.ShapeDtypeStruct((16, 128), F32),
        ],
        compiler_params=pltpu.CompilerParams(vmem_limit_bytes=24 * 2**20),
        cost_estimate=pl.CostEstimate(flops=900_000_000, bytes_accessed=3_000_000, transcendentals=0),
    )(tile_vec, conv_in, conv_mid, conv_out)


def field_kernel(tile_ref, lat_ref, basis_ref, prev_ref, src_ref, field_ref, near_ref, far_ref, held, sems):
    chunks, comps, layers, rows, width = held.shape
    members, total = lat_ref.shape
    span = comps * rows
    copies = [
        pltpu.make_async_copy(basis_ref.at[pl.ds(c * comps, comps)], held.at[c], sems.at[c]) for c in range(chunks)
    ]
    for copy in copies:
        copy.start()
    lat = lat_ref[...].astype(BF)
    own = iota((rows, span), 0) == iota((rows, span), 1) & (rows - 1)
    behind = iota((total, span), 0) - split(iota((total, span), 1), rows)[0]
    for c in range(chunks):
        pick = jnp.where(behind == c * comps, 1.0, 0.0).astype(BF)
        spread = jnp.dot(lat, pick, preferred_element_type=F32)
        left = jnp.where(own[None], spread[:, None, :], 0.0).astype(BF).reshape(members * rows, span)
        copies[c].wait()
        for z in range(layers):
            part = jnp.dot(left, held[c, :, z].reshape(span, width), preferred_element_type=F32)
            part = part.reshape(members, rows, width)
            field_ref[z] = part if c == 0 else field_ref[z] + part
    tiles = [field_ref.at[z, m] for z in range(layers) for m in range(members)]
    tiles += [prev_ref.at[z] for z in range(layers)] + [src_ref.at[z] for z in range(layers)]
    first = iota((8, width), 0) < HALO
    even_tile = tile_ref[0] & 1 == 0
    for pair in range(len(tiles) // 2):
        even, odd = tiles[2 * pair], tiles[2 * pair + 1]
        low = jnp.where(first, even[0:8], pltpu.roll(odd[0:8], HALO, 0))
        high = jnp.where(first, pltpu.roll(odd[rows - 8 : rows], HALO, 0), even[rows - 8 : rows])
        near_ref[pair] = jnp.where(even_tile, high, low)
        far_ref[pair] = jnp.where(even_tile, low, high)


def field_of(tile_vec, latents, basis, prev, src):
    total, layers, rows, width = basis.shape
    members = latents.shape[0]
    comps = 32
    pairs = (layers * members + 2 * layers) // 2
    return pl.pallas_call(
        field_kernel,
        in_specs=[SMEM, VMEM, pl.BlockSpec(memory_space=pl.ANY), VMEM, VMEM],
        out_specs=[VMEM] * 3,
        out_shape=[
            jax.ShapeDtypeStruct((layers, members, rows, width), F32),
            jax.ShapeDtypeStruct((pairs, 8, width), F32),
            jax.ShapeDtypeStruct((pairs, 8, width), F32),
        ],
        scratch_shapes=[
            pltpu.VMEM((total // comps, comps, layers, rows, width), BF),
            pltpu.SemaphoreType.DMA((total // comps,)),
        ],
        compiler_params=pltpu.CompilerParams(vmem_limit_bytes=58 * 2**20),
    )(tile_vec, latents, basis, prev, src)


def target(me, k, count):
    return (me + k) % count if count & (count - 1) else me ^ k


def origin(me, k, count):
    return (me + count - k) % count if count & (count - 1) else me ^ k


def split(value, by):
    if by & (by - 1):
        return value // by, value % by
    return value >> (by.bit_length() - 1), value & (by - 1)


def decode_kernel(
    grid_rows,
    tile_ref,
    mem_ref,
    field_ref,
    near_ref,
    far_ref,
    prev_ref,
    src_ref,
    win_ref,
    wmix_ref,
    gain_ref,
    ids_ref,
    count_ref,
    *refs,

):
    parts = len(refs) - 10
    press_refs, sums_ref = refs[:parts], refs[parts]
    f_scr, t_scr, pt_scr, lift_scr, side_scr, deep_scr, wout_scr, v_scr, press_scr = refs[parts + 1 :]
    layers, members, rows, width = field_ref.shape
    groups = layers * members
    steps = width // (2 * SEG)
    block_rows = width // 2
    tile, mem = tile_ref[0], mem_ref[0]
    even_tile = tile & 1 == 0

    def outer(pair):
        near, far = near_ref[pair], far_ref[pair]
        up, down = jnp.where(even_tile, near, far), jnp.where(even_tile, far, near)
        first = iota(up.shape, 0) < HALO
        return jnp.where(first, up, down), pltpu.roll(jnp.where(first, down, up), HALO, 0)

    def load(pair, _):
        thirds = outer(pair)
        for half in range(2):
            group = 2 * pair + half
            own = field_ref[group // members, lax.rem(group, members)]
            f = jnp.concatenate([own, thirds[half]], axis=0)
            f_scr[group] = f
            hi = f.astype(BF).astype(F32)
            lo = f - hi
            zero = jnp.zeros((32 - RING, width), F32)
            edge = iota((RING, width), 1) == 0
            hi_left = jnp.where(edge, 0.0, pltpu.roll(hi, 1, 1))
            lo_left = jnp.where(edge, 0.0, pltpu.roll(lo, 1, 1))
            tall = jnp.concatenate([hi_left, zero, lo_left, zero, hi, zero, lo, zero], axis=0).T
            t_scr[0:width, :] = tall
            end = pltpu.roll(tall[width - 8 : width], 64, 1)
            end = jnp.where(iota(end.shape, 1) < 64, end, 0.0)
            t_scr[width : width + 8, :] = pltpu.roll(end, 1, 0)
            for q in range(steps + 1):
                part = t_scr[pl.ds(2 * q, SEG, stride=2 * steps), :].astype(BF)
                if q < steps:
                    pt_scr[pl.ds(pl.multiple_of(group * block_rows + q * SEG, SEG), SEG), 0:128] = part
                if q > 0:
                    pt_scr[pl.ds(pl.multiple_of(group * block_rows + (q - 1) * SEG, SEG), SEG), 128:256] = part
        return 0

    lax.fori_loop(0, groups // 2, load, 0)

    chunk = CHUNK_GROUPS * block_rows
    chunks = groups * block_rows // chunk

    def lift(t, _):
        block, part = t // chunks, lax.rem(t, chunks)
        at = pl.multiple_of(part * chunk, chunk)
        wide = jnp.dot(pt_scr[pl.ds(at, chunk), :], win_ref[block], preferred_element_type=F32)
        wide = jnp.maximum(wide, 0.0)
        tight = wide.astype(BF)
        lift_scr[block, pl.ds(at, chunk), :] = tight
        right = iota((SEG, 256), 1) & 64 == 0
        row = iota((SEG, 256), 0)
        for i in range(chunk // block_rows):
            base = i * block_rows
            last = base + block_rows - SEG
            after = jnp.where(row < SEG - 1, pltpu.roll(wide[base : base + SEG], SEG - 1, 0), 0.0)
            before = jnp.where(row > 0, pltpu.roll(wide[last : last + SEG], 1, 0), 0.0)
            for q in range(steps):
                r = base + q * SEG
                nxt = after if q == steps - 1 else wide[r + SEG : r + 2 * SEG]
                prv = before if q == 0 else wide[r - SEG : r]
                side_scr[block, pl.ds(pl.multiple_of(at + r, SEG), SEG), :] = jnp.where(right, nxt, prv).astype(BF)
        return 0


    gain0, gain1 = gain_ref[0:1, :], gain_ref[8:9, :]

    def mix(t, _):
        block, part = t // chunks + 1, lax.rem(t, chunks)
        above = block - 1
        below = jnp.where(block == LIFT_BLOCKS - 1, 0, block + 1)
        at = pl.ds(pl.multiple_of(part * chunk, chunk), chunk)
        x = jnp.concatenate(
            [
                lift_scr[block, at, :],
                side_scr[block, at, :],
                lift_scr[below, at, 0:128],
                lift_scr[above, at, 128:256],
                side_scr[below, at, 0:128],
                side_scr[above, at, 128:256],
            ],
            axis=1,
        )
        deep = jnp.maximum(jnp.dot(x, wmix_ref[...], preferred_element_type=F32), 0.0)
        deep_scr[block - 1, at, :] = (deep[:, :128] * gain0 + deep[:, 128:] * gain1).astype(BF)
        return 0

    def both_steps(t, _):
        mix(t, 0)
        lift(t + 3 * chunks, 0)
        return 0

    lax.fori_loop(0, 3 * chunks, lift, 0)
    lax.fori_loop(0, (LIFT_BLOCKS - 3) * chunks, both_steps, 0)
    lax.fori_loop((LIFT_BLOCKS - 3) * chunks, MIX_BLOCKS * chunks, mix, 0)

    k, n = iota(wout_scr.shape, 0), iota(wout_scr.shape, 1)
    place = (k & 127) >> 5
    row = 2 * ((k >> 7) + 1) - HALO + (place >> 1)
    row = jnp.where(row < 0, row + RING, row)
    wout_scr[...] = jnp.where(n == (place & 1) * 32 + row, 1.0, 0.0).astype(BF)

    def collect(pair, _):
        at = pl.ds(pl.multiple_of(pair * 2 * block_rows, 2 * block_rows), 2 * block_rows)
        x = jnp.concatenate([deep_scr[j, at, :] for j in range(MIX_BLOCKS)], axis=1)
        both = jnp.dot(x, wout_scr[...], preferred_element_type=F32)
        both = both[:block_rows] + pltpu.roll(both[block_rows:], 64, 1)
        for q in range(steps):
            part = both[q * SEG : (q + 1) * SEG]
            t_scr[pl.ds(2 * q, SEG, stride=2 * steps), :] = part
            t_scr[pl.ds(2 * q + 1, SEG, stride=2 * steps), :] = part
        flat = t_scr[0:width, :].T
        even = iota((RING, width), 1) & 1 == 0
        for half in range(2):
            s = 64 * half
            f_scr[2 * pair + half] = f_scr[2 * pair + half] + jnp.where(
                even, flat[s : s + RING], flat[s + 32 : s + 32 + RING]
            )
        return 0

    lax.fori_loop(0, groups // 2, collect, 0)

    full = (RING, width)
    ring = iota(full, 0)
    grid_row = tile * rows + jnp.where(ring < rows + HALO, ring, ring - RING)
    inside = (grid_row >= 0) & (grid_row < grid_rows)
    joined = (grid_row >= 0) & (grid_row < grid_rows - 1)
    not_last = iota(full, 1) < width - 1

    def ring_of(ref, group, z):
        return jnp.concatenate([ref[z], outer(group // 2)[group % 2]], axis=0)

    def row_next(v):
        return pltpu.roll(v, RING - 1, 0)

    def row_prev(v):
        return pltpu.roll(v, 1, 0)

    def col_next(v):
        return pltpu.roll(v, width - 1, 1)

    def col_prev(v):
        return pltpu.roll(v, 1, 1)

    start = [ring_of(prev_ref, groups + z, z) for z in range(layers)]
    base = [start[z] + ring_of(src_ref, groups + layers + z, z) for z in range(layers)]
    around = [[f(start[z]) for f in (row_next, row_prev, col_next, col_prev)] for z in range(layers)]

    def flow(p, q):
        return 2.0 * p * q / (p + q)

    def sweep(member, _):
        perm = [jnp.where(inside, jnp.exp(f_scr[z * members + member]), 1.0) for z in range(layers)]
        between = jnp.where(inside, flow(perm[0], perm[1]), 0.0)
        faces, scale = [], []
        for z in range(layers):
            below = jnp.where(joined, flow(perm[z], row_next(perm[z])), 0.0)
            right = jnp.where(not_last, flow(perm[z], col_next(perm[z])), 0.0)
            right = jnp.where(inside, right, 0.0)
            face = (below, row_prev(below), right, col_prev(right))
            faces.append(face)
            scale.append(1.0 / (1.0 + between + face[0] + face[1] + face[2] + face[3]))
        press, near = start, around
        for turn in range(SWEEPS):
            if turn > 0:
                near = [[f(press[z]) for f in (row_next, row_prev, col_next, col_prev)] for z in range(layers)]
            press = [
                (base[z] + between * press[1 - z] + sum(c * v for c, v in zip(faces[z], near[z]))) * scale[z]
                for z in range(layers)
            ]
        cols = width // parts
        for z in range(layers):
            press_scr[...] = press[z][:rows]
            for k in range(parts):
                at = pl.multiple_of(target(mem, k, parts) * cols, cols)
                press_refs[k][member, z] = press_scr[:, pl.ds(at, cols)]
            weight = perm[z][:rows]
            for kind, value in enumerate((weight * press[z][:rows], weight)):
                hi = value.astype(BF)
                lo = (value - hi.astype(F32)).astype(BF)
                for part, piece in enumerate((hi, lo)):
                    at = (((kind * 2 + part) * members + member) * layers + z) * rows
                    v_scr[pl.ds(pl.multiple_of(at, rows), rows), :] = piece
        return 0

    lax.fori_loop(0, members, sweep, 0)

    slots, wells = ids_ref.shape
    cells = layers * rows
    layer_at, rest = split(ids_ref[...], grid_rows * width)
    row_at, col = split(rest, width)
    row_at = row_at - tile * rows
    used = (iota((slots, wells), 0) < count_ref[...]) & (row_at >= 0) & (row_at < rows)
    sel = jnp.where(used, layer_at * rows + row_at, -1)
    sums = jnp.zeros((4 * members, wells), F32)
    for slot in range(0, slots, 2):
        sel_two = jnp.concatenate([sel[slot : slot + 1], sel[slot + 1 : slot + 2]], axis=1)
        col_two = jnp.concatenate([col[slot : slot + 1], col[slot + 1 : slot + 2]], axis=1)
        here = iota((width, 2 * wells), 0) == col_two
        got = jnp.dot(v_scr[...], jnp.where(here, 1.0, 0.0).astype(BF), preferred_element_type=F32)
        mine = iota((cells, 2 * wells), 0) == sel_two
        picked = jnp.where(mine[None], got.reshape(4 * members, cells, 2 * wells), 0.0)
        both = jnp.sum(picked, axis=1)
        sums = sums + both[:, :wells] + both[:, wells:]
    sums_ref[0:members] = sums[0:members] + sums[members : 2 * members]
    sums_ref[members : 2 * members] = sums[2 * members : 3 * members] + sums[3 * members :]


def decode(parts, tile_vec, mem_vec, grid_rows, field, near, far, prev, src, win, wmix, gains, ids, counts):
    layers, members, rows, width = field.shape
    groups = layers * members
    total = groups * width // 2
    wells = ids.shape[1]
    return pl.pallas_call(
        functools.partial(decode_kernel, grid_rows),
        in_specs=[SMEM] * 2 + [VMEM] * 10,
        out_specs=[VMEM] * (parts + 1),
        out_shape=[jax.ShapeDtypeStruct((members, layers, rows, width // parts), F32)] * parts
        + [jax.ShapeDtypeStruct((2 * members, wells), F32)],
        scratch_shapes=[
            pltpu.VMEM((groups, RING, width), F32),
            pltpu.VMEM((width + 8, 128), F32),
            pltpu.VMEM((total, 256), BF),
            pltpu.VMEM((LIFT_BLOCKS, total, 256), BF),
            pltpu.VMEM((LIFT_BLOCKS, total, 256), BF),
            pltpu.VMEM((MIX_BLOCKS, total, 128), BF),
            pltpu.VMEM((MIX_BLOCKS * 128, 128), BF),
            pltpu.VMEM((4 * groups * rows, width), BF),
            pltpu.VMEM((rows, width), F32),
        ],
        compiler_params=pltpu.CompilerParams(vmem_limit_bytes=52 * 2**20),
    )(tile_vec, mem_vec, field, near, far, prev, src, win, wmix, gains, ids, counts)


def update_kernel(mem_ref, refs, swap_refs, obs_ref, err_ref, press_ref, data_ref, new_ref, all_scr, step_scr):
    count = len(refs)
    own = refs[0].shape[0]
    members, wells = obs_ref.shape
    mem = mem_ref[0]
    for k in range(count):
        source = origin(mem, k, count)
        all_scr[source] = refs[k][...]
        press_ref[source] = swap_refs[k][...]
    every = jnp.concatenate([all_scr[k] for k in range(count)], axis=0)
    data, every = every[:, :wells], every[:, wells:]
    data_ref[...] = data
    scale = 2.0 * err_ref[...]
    root = math.sqrt(members - 1)
    scaled = (data - jnp.mean(data, axis=0, keepdims=True)) / (root * scale)
    innov = (obs_ref[...] - data) / scale
    dims = (((1,), (1,)), ((), ()))
    exact = lax.Precision.HIGHEST
    eye = (iota((members, members), 0) == iota((members, members), 1)).astype(F32)
    gram = eye + lax.dot_general(scaled, scaled, dims, precision=exact, preferred_element_type=F32)
    cross = lax.dot_general(innov, scaled, dims, precision=exact, preferred_element_type=F32)
    right = (every - jnp.mean(every, axis=0, keepdims=True)) / root
    place = iota((members, 1), 0)
    for k in range(members):
        inverse = 1.0 / gram[k : k + 1, k : k + 1]
        factor = jnp.where(place == k, 0.0, gram[:, k : k + 1])
        gram_row = gram[k : k + 1, :] * inverse
        right_row = right[k : k + 1, :] * inverse
        gram = jnp.where(place == k, gram_row, gram - factor * gram_row)
        right = jnp.where(place == k, right_row, right - factor * right_row)
    new = every + jnp.dot(cross, right, precision=exact, preferred_element_type=F32)
    for k in range(count):
        step_scr[k] = new[k * own : (k + 1) * own]
    new_ref[...] = step_scr[mem]


def update(mem_vec, pieces, swaps, obs, err):
    count = len(pieces)
    own, total = pieces[0].shape
    members, wells = obs.shape

    def kernel(mem_ref, *refs):
        update_kernel(mem_ref, refs[:count], refs[count : 2 * count], *refs[2 * count :])

    return pl.pallas_call(
        kernel,
        in_specs=[SMEM] + [VMEM] * (2 * count + 2),
        out_specs=[VMEM] * 3,
        out_shape=[
            jax.ShapeDtypeStruct((count,) + swaps[0].shape, F32),
            jax.ShapeDtypeStruct((members, wells), F32),
            jax.ShapeDtypeStruct((own, total - wells), F32),
        ],
        scratch_shapes=[
            pltpu.VMEM((count, own, total), F32),
            pltpu.VMEM((count, own, total - wells), F32),
        ],
        compiler_params=pltpu.CompilerParams(vmem_limit_bytes=24 * 2**20),
    )(mem_vec, *pieces, *swaps, obs, err)


def gathered(pieces, axis):
    count = lax.axis_size(axis)
    return [pieces[0]] + [
        lax.ppermute(pieces[k], axis, [(i, target(i, k, count)) for i in range(count)]) for k in range(1, count)
    ]


def summed(own, axis):
    count = lax.axis_size(axis)
    if count & (count - 1):
        return lax.psum(own, axis)
    k = 1
    while k < count:
        jumps = (k, 2 * k, 3 * k) if 4 * k <= count else (k,)
        own = own + sum(lax.ppermute(own, axis, [(i, i ^ j) for i in range(count)]) for j in jumps)
        k *= len(jumps) + 1
    return own


def halo(near, far, axis):
    count = lax.axis_size(axis)
    swap = lambda first: [p for i in range(first, count - 1, 2) for p in ((i, i + 1), (i + 1, i))]
    far = lax.ppermute(far, axis, swap(1))
    return lax.ppermute(near, axis, swap(0)), far


def body(
    latents,
    basis,
    conv_in,
    conv_mid,
    conv_out,
    pressure_prev,
    source,
    perf_cells,
    perf_count,
    obs_perturbed,
    obs_error,
):
    members = latents.shape[0]
    layers, rows, width = basis.shape[1:]
    tiles = lax.axis_size("tile")
    parts = lax.axis_size("mem")
    grid_rows = rows * tiles
    tile_vec = lax.axis_index("tile").astype(jnp.int32).reshape(1)
    mem_vec = lax.axis_index("mem").astype(jnp.int32).reshape(1)

    field, near, far = field_of(tile_vec, latents, basis, pressure_prev, source)
    near, far = halo(near, far, "tile")
    win, wmix, gains = placed(tile_vec, grid_rows, rows, conv_in, conv_mid, conv_out.reshape(1, -1))
    *press, sums = decode(
        parts, tile_vec, mem_vec, grid_rows, field, near, far, pressure_prev, source,
        win, wmix, gains, perf_cells.T, perf_count.reshape(1, -1),
    )
    swaps = gathered(press, "mem")
    sums = summed(sums, "tile")
    well = jnp.concatenate([sums[:members] / sums[members:], latents], axis=1)
    pieces = gathered([well] * parts, "mem")
    press, data, new = update(mem_vec, pieces, swaps, obs_perturbed, obs_error.reshape(1, -1))
    return (press.reshape((parts * members,) + press.shape[2:]), data, new)


def solution(mesh):
    return jax.shard_map(
        body,
        mesh=mesh,
        in_specs=(
            P("mem", None),
            P(None, None, "tile", None),
            P(),
            P(),
            P(),
            P(None, "tile", None),
            P(None, "tile", None),
            P(),
            P(),
            P(),
            P(),
        ),
        out_specs=(P(None, None, "tile", "mem"), P(), P("mem", None)),
        check_vma=False,
    )
```

```python
import functools
import math

import jax
import jax.numpy as jnp
from jax import lax
from jax.experimental import pallas as pl
from jax.experimental.pallas import tpu as pltpu
from jax.sharding import PartitionSpec as P

SWEEPS = 2
PACKED = 96
HALO = 4
RING = 24
LIFT_BLOCKS = 11
HELD = 5
MIX_BLOCKS = 10
CHUNK_GROUPS = 12
SEG = 16
BF = jnp.bfloat16
F32 = jnp.float32
VMEM = pl.BlockSpec(memory_space=pltpu.VMEM)
SMEM = pl.BlockSpec(memory_space=pltpu.SMEM)


def iota(shape, dim):
    return lax.broadcasted_iota(jnp.int32, shape, dim)


def place_weights(tile, grid_rows, rows, in_ref, mid_ref, out_ref, win_ref, wmix_ref, gain_ref):
    one = lambda mask: jnp.where(mask, 1.0, 0.0).astype(BF)
    dot = functools.partial(jnp.dot, preferred_element_type=F32)
    taps = dot(one(iota((64, 9), 0) & 15 == iota((64, 9), 1)), in_ref[...]).astype(BF)
    taps = dot(taps, one(iota((64, 256), 0) == iota((64, 256), 1) & 63))
    kinds = jnp.where(iota((64, 256), 0) >> 4 == iota((64, 256), 1) >> 6, taps, 0.0).astype(BF)
    k, j = iota((256, 64), 0), iota((256, 64), 1)
    offset, ring = k >> 6, k & 31
    place, tap = j >> 4, j & 15
    xx, yy = place >> 1, place & 1
    a = ((tap * 11) >> 5) - 1
    b = tap - 3 * (a + 1) - 1
    fits = (tap < 9) & (offset == yy + b + 1)
    for block in range(LIFT_BLOCKS):
        row = jnp.where(xx == 0, 18, -3) if block == 0 else 2 * block - HALO + xx
        near = row + a
        near = jnp.where(near < 0, near + RING, near)
        grid_row = tile * rows + row
        pick = fits & (ring == near) & (grid_row >= 0) & (grid_row < grid_rows)
        win_ref[block] = dot(one(pick), kinds).astype(BF)
    o, n = iota((64, 1024), 0), iota((64, 1024), 1)
    put = one(n & 255 == (o >> 5) * 128 + (n >> 8) * 32 + (o & 31))
    placed = [
        lax.dot_general(mid_ref[t], put, (((0,), (0,)), ((), ())), preferred_element_type=F32) for t in range(9)
    ]
    for kind in range(4):
        side, over = kind & 1, kind >> 1
        for place_in in range(4):
            xi, yi = place_in >> 1, place_in & 1
            total = jnp.zeros((64, 256), F32)
            for place_out in range(4):
                xo, yo = place_out >> 1, place_out & 1
                dx = xi - xo + (0 if not over else (2 if xi == 0 else -2))
                dy = yi - yo + (0 if not side else (2 if yi == 0 else -2))
                if abs(dx) <= 1 and abs(dy) <= 1:
                    t = 3 * (dx + 1) + dy + 1
                    total = total + placed[t][:, 256 * place_out : 256 * place_out + 256]
            at = 256 * kind + 64 * place_in
            wmix_ref[at : at + 64, :] = total.astype(BF)
    gains = jnp.broadcast_to(out_ref[...].astype(F32), (8, 64)).astype(BF)
    c, n = iota((64, 128), 0), iota((64, 128), 1)
    gain_ref[0:8] = dot(gains, one(c == n & 31))
    gain_ref[8:16] = dot(gains, one(c == 32 + (n & 31)))


def place_kernel(grid_rows, rows, tile_ref, in_ref, mid_ref, out_ref, win_ref, wmix_ref, gain_ref):
    place_weights(tile_ref[0], grid_rows, rows, in_ref, mid_ref, out_ref, win_ref, wmix_ref, gain_ref)


def placed(tile_vec, grid_rows, rows, conv_in, conv_mid, conv_out):
    return pl.pallas_call(
        functools.partial(place_kernel, grid_rows, rows),
        in_specs=[SMEM] + [VMEM] * 3,
        out_specs=[VMEM] * 3,
        out_shape=[
            jax.ShapeDtypeStruct((LIFT_BLOCKS, 256, 256), BF),
            jax.ShapeDtypeStruct((1024, 256), BF),
            jax.ShapeDtypeStruct((16, 128), F32),
        ],
        compiler_params=pltpu.CompilerParams(vmem_limit_bytes=24 * 2**20),
        cost_estimate=pl.CostEstimate(flops=900_000_000, bytes_accessed=3_000_000, transcendentals=0),
    )(tile_vec, conv_in, conv_mid, conv_out)


def field_kernel(tile_ref, lat_ref, basis_ref, prev_ref, src_ref, field_ref, near_ref, far_ref, held, sems):
    chunks, comps, layers, rows, width = held.shape
    members, total = lat_ref.shape
    span = comps * rows
    copies = [
        pltpu.make_async_copy(basis_ref.at[pl.ds(c * comps, comps)], held.at[c], sems.at[c]) for c in range(chunks)
    ]
    for copy in copies:
        copy.start()
    even_tile = tile_ref[0] & 1 == 0
    shape = (PACKED, 2 * (layers * members + 2 * layers) * rows)
    picks = [packed_from(layers, members, rows, up, shape) for up in (even_tile, jnp.logical_not(even_tile))]
    lat = lat_ref[...].astype(BF)
    own = iota((rows, span), 0) == iota((rows, span), 1) & (rows - 1)
    behind = iota((total, span), 0) - split(iota((total, span), 1), rows)[0]
    for c in range(chunks):
        pick = jnp.where(behind == c * comps, 1.0, 0.0).astype(BF)
        spread = jnp.dot(lat, pick, preferred_element_type=F32)
        left = jnp.where(own[None], spread[:, None, :], 0.0).astype(BF).reshape(members * rows, span)
        copies[c].wait()
        for z in range(layers):
            part = jnp.dot(left, held[c, :, z].reshape(span, width), preferred_element_type=F32)
            part = part.reshape(members, rows, width)
            field_ref[z] = part if c == 0 else field_ref[z] + part
    exact, rest = [], []
    for value in (field_ref[...].reshape(-1, width), prev_ref[...].reshape(-1, width), src_ref[...].reshape(-1, width)):
        hi = value.astype(BF)
        exact.append(hi)
        rest.append((value - hi.astype(F32)).astype(BF))
    pool = jnp.concatenate([exact[0], rest[0], exact[1], rest[1], exact[2], rest[2]], axis=0)
    for ref, pick in zip((near_ref, far_ref), picks):
        ref[...] = jnp.dot(pick, pool, preferred_element_type=F32).astype(BF)


def packed_from(layers, members, rows, upper, shape):
    groups = layers * members
    r, at = iota((shape[0], 1), 0), iota(shape, 1)
    last = jnp.where(upper, 1, 0)
    group = (r * 43) >> 8
    j = r - 6 * group
    row_hi = jnp.where(last == 1, rows - HALO + j, j)
    row_lo = jnp.where(last == 1, rows - 2 + j - HALO, j - HALO)
    field = jnp.where(j < HALO, group * rows + row_hi, (groups + group) * rows + row_lo)
    p = r - 6 * groups
    half, j = (p >> 1) & 1, p & 1
    prev = (2 * groups + half * layers + (p >> 2)) * rows + jnp.where(last == 1, rows - 2 + j, j)
    s = p - 4 * layers
    src = (2 * groups + (2 + (s & 1)) * layers + (s >> 1)) * rows + jnp.where(last == 1, rows - 1, 0)
    wanted = jnp.where(p < 0, field, jnp.where(s < 0, prev, jnp.where(s < 2 * layers, src, -1)))
    return jnp.where(wanted == at, 1.0, 0.0).astype(BF)


def unpacked_to(layers, members, upper, shape):
    groups = layers * members
    r, at = iota((shape[0], 1), 0), iota(shape, 1)
    group, s = r >> 3, r & 7
    up = jnp.where(upper, 1, 0)
    j = jnp.where(up == 1, s - HALO, s)
    mine = (j >= 0) & (j < HALO)
    near = jnp.where(up == 1, j - 2, j)
    close = mine & (near >= 0) & (near < 2)
    z = group - groups
    hi = jnp.where(z < 0, group * 6 + j, 6 * groups + z * 4 + near)
    lo = jnp.where(z < 0, group * 6 + HALO + near, 6 * groups + z * 4 + 2 + near)
    is_src = z >= layers
    src = 6 * groups + 4 * layers + 2 * (z - layers)
    edge = close & (jnp.where(up == 1, near, 1 - near) == 1)
    hi = jnp.where(is_src, src, hi)
    lo = jnp.where(is_src, src + 1, lo)
    use_hi = (z < 0) & mine | (z >= 0) & (z < layers) & close | is_src & edge
    use_lo = (z < layers) & close | is_src & edge
    return jnp.where(use_hi & (at == hi) | use_lo & (at == lo), 1.0, 0.0).astype(BF)


def field_of(tile_vec, latents, basis, prev, src):
    total, layers, rows, width = basis.shape
    members = latents.shape[0]
    comps = 32
    return pl.pallas_call(
        field_kernel,
        in_specs=[SMEM, VMEM, pl.BlockSpec(memory_space=pltpu.HBM), VMEM, VMEM],
        out_specs=[VMEM] * 3,
        out_shape=[
            jax.ShapeDtypeStruct((layers, members, rows, width), F32),
            jax.ShapeDtypeStruct((PACKED, width), BF),
            jax.ShapeDtypeStruct((PACKED, width), BF),
        ],
        scratch_shapes=[
            pltpu.VMEM((total // comps, comps, layers, rows, width), BF),
            pltpu.SemaphoreType.DMA((total // comps,)),
        ],
        compiler_params=pltpu.CompilerParams(vmem_limit_bytes=57 * 2**20),
    )(tile_vec, latents, basis, prev, src)


def target(me, k, count):
    return (me + k) % count if count & (count - 1) else me ^ k


def origin(me, k, count):
    return (me + count - k) % count if count & (count - 1) else me ^ k


def split(value, by):
    if by & (by - 1):
        return value // by, value % by
    return value >> (by.bit_length() - 1), value & (by - 1)


def decode_kernel(
    grid_rows,
    tile_ref,
    mem_ref,
    field_ref,
    near_ref,
    far_ref,
    prev_ref,
    src_ref,
    win_ref,
    wmix_ref,
    gain_ref,
    ids_ref,
    count_ref,
    *refs,

):
    parts = len(refs) - 11
    press_refs, sums_ref = refs[:parts], refs[parts]
    f_scr, t_scr, pt_scr, lift_scr, side_scr, deep_scr, wout_scr, v_scr, press_scr, third_scr = refs[parts + 1 :]
    layers, members, rows, width = field_ref.shape
    groups = layers * members
    steps = width // (2 * SEG)
    block_rows = width // 2
    tile, mem = tile_ref[0], mem_ref[0]
    even_tile = tile & 1 == 0

    shape = ((groups + 2 * layers) * 8, PACKED)
    from_near = unpacked_to(layers, members, jnp.logical_not(even_tile), shape)
    from_far = unpacked_to(layers, members, even_tile, shape)
    third_scr[...] = (
        jnp.dot(from_near, near_ref[...], preferred_element_type=F32)
        + jnp.dot(from_far, far_ref[...], preferred_element_type=F32)
    ).reshape(-1, 8, width)

    def load(pair, _):
        for half in range(2):
            group = 2 * pair + half
            own = field_ref[group // members, lax.rem(group, members)]
            f = jnp.concatenate([own, third_scr[group]], axis=0)
            f_scr[group] = f
            hi = f.astype(BF).astype(F32)
            lo = f - hi
            zero = jnp.zeros((32 - RING, width), F32)
            edge = iota((RING, width), 1) == 0
            hi_left = jnp.where(edge, 0.0, pltpu.roll(hi, 1, 1))
            lo_left = jnp.where(edge, 0.0, pltpu.roll(lo, 1, 1))
            tall = jnp.concatenate([hi_left, zero, lo_left, zero, hi, zero, lo, zero], axis=0).T
            t_scr[half, 0:width, :] = tall
            end = pltpu.roll(tall[width - 8 : width], 64, 1)
            end = jnp.where(iota(end.shape, 1) < 64, end, 0.0)
            t_scr[half, width : width + 8, :] = pltpu.roll(end, 1, 0)
            for q in range(steps + 1):
                part = t_scr[half, pl.ds(2 * q, SEG, stride=2 * steps), :].astype(BF)
                if q < steps:
                    pt_scr[pl.ds(pl.multiple_of(group * block_rows + q * SEG, SEG), SEG), 0:128] = part
                if q > 0:
                    pt_scr[pl.ds(pl.multiple_of(group * block_rows + (q - 1) * SEG, SEG), SEG), 128:256] = part
        return 0

    lax.fori_loop(0, groups // 2, load, 0)

    chunk = CHUNK_GROUPS * block_rows
    chunks = groups * block_rows // chunk

    def slot_of(block):
        return jnp.where(block == 0, 0, 1 + lax.rem(block + HELD - 1, HELD))

    def lift(t, _):
        block, part = t // chunks, lax.rem(t, chunks)
        slot = slot_of(block)
        at = pl.multiple_of(part * chunk, chunk)
        wide = jnp.dot(pt_scr[pl.ds(at, chunk), :], win_ref[block], preferred_element_type=F32)
        wide = jnp.maximum(wide, 0.0)
        tight = wide.astype(BF)
        lift_scr[slot, pl.ds(at, chunk), :] = tight
        right = iota((SEG, 256), 1) & 64 == 0
        row = iota((SEG, 256), 0)
        for i in range(chunk // block_rows):
            base = i * block_rows
            last = base + block_rows - SEG
            after = jnp.where(row < SEG - 1, pltpu.roll(wide[base : base + SEG], SEG - 1, 0), 0.0)
            before = jnp.where(row > 0, pltpu.roll(wide[last : last + SEG], 1, 0), 0.0)
            for q in range(steps):
                r = base + q * SEG
                nxt = after if q == steps - 1 else wide[r + SEG : r + 2 * SEG]
                prv = before if q == 0 else wide[r - SEG : r]
                side_scr[slot, pl.ds(pl.multiple_of(at + r, SEG), SEG), :] = jnp.where(right, nxt, prv).astype(BF)
        return 0


    gain0, gain1 = gain_ref[0:1, :], gain_ref[8:9, :]

    def mix(t, _):
        block, part = t // chunks + 1, lax.rem(t, chunks)
        above = slot_of(block - 1)
        below = slot_of(jnp.where(block == LIFT_BLOCKS - 1, 0, block + 1))
        here = slot_of(block)
        at = pl.ds(pl.multiple_of(part * chunk, chunk), chunk)
        x = jnp.concatenate(
            [
                lift_scr[here, at, :],
                side_scr[here, at, :],
                lift_scr[below, at, 0:128],
                lift_scr[above, at, 128:256],
                side_scr[below, at, 0:128],
                side_scr[above, at, 128:256],
            ],
            axis=1,
        )
        deep = jnp.maximum(jnp.dot(x, wmix_ref[...], preferred_element_type=F32), 0.0)
        deep_scr[block - 1, at, :] = (deep[:, :128] * gain0 + deep[:, 128:] * gain1).astype(BF)
        return 0

    def both_steps(t, _):
        mix(t, 0)
        lift(t + 3 * chunks, 0)
        return 0

    lax.fori_loop(0, 3 * chunks, lift, 0)
    lax.fori_loop(0, (LIFT_BLOCKS - 3) * chunks, both_steps, 0)
    lax.fori_loop((LIFT_BLOCKS - 3) * chunks, MIX_BLOCKS * chunks, mix, 0)

    k, n = iota(wout_scr.shape, 0), iota(wout_scr.shape, 1)
    place = (k & 127) >> 5
    row = 2 * ((k >> 7) + 1) - HALO + (place >> 1)
    row = jnp.where(row < 0, row + RING, row)
    wout_scr[...] = jnp.where(n == (place & 1) * 32 + row, 1.0, 0.0).astype(BF)

    def collect(pair, held):
        at = pl.ds(pl.multiple_of(pair * 2 * block_rows, 2 * block_rows), 2 * block_rows)
        x = jnp.concatenate([deep_scr[j, at, :] for j in range(MIX_BLOCKS)], axis=1)
        both = jnp.dot(x, wout_scr[...], preferred_element_type=F32)
        both = both[:block_rows] + pltpu.roll(both[block_rows:], 64, 1)
        for q in range(steps):
            part = both[q * SEG : (q + 1) * SEG]
            t_scr[held, pl.ds(2 * q, SEG, stride=2 * steps), :] = part
            t_scr[held, pl.ds(2 * q + 1, SEG, stride=2 * steps), :] = part
        flat = t_scr[held, 0:width, :].T
        even = iota((RING, width), 1) & 1 == 0
        for half in range(2):
            s = 64 * half
            f_scr[2 * pair + half] = f_scr[2 * pair + half] + jnp.where(
                even, flat[s : s + RING], flat[s + 32 : s + 32 + RING]
            )

    for pair in range(groups // 2):
        collect(pair, pair)

    full = (RING, width)
    ring = iota(full, 0)
    grid_row = tile * rows + jnp.where(ring < rows + HALO, ring, ring - RING)
    inside = (grid_row >= 0) & (grid_row < grid_rows)
    joined = (grid_row >= 0) & (grid_row < grid_rows - 1)
    not_last = iota(full, 1) < width - 1

    def ring_of(ref, group, z):
        return jnp.concatenate([ref[z], third_scr[group]], axis=0)

    def row_next(v):
        return pltpu.roll(v, RING - 1, 0)

    def row_prev(v):
        return pltpu.roll(v, 1, 0)

    def col_next(v):
        return pltpu.roll(v, width - 1, 1)

    def col_prev(v):
        return pltpu.roll(v, 1, 1)

    start = [ring_of(prev_ref, groups + z, z) for z in range(layers)]
    base = [start[z] + ring_of(src_ref, groups + layers + z, z) for z in range(layers)]
    around = [[f(start[z]) for f in (row_next, row_prev, col_next, col_prev)] for z in range(layers)]

    def flow(p, q):
        return 2.0 * p * q / (p + q)

    def sweep(member, _):
        perm = [jnp.where(inside, jnp.exp(f_scr[z * members + member]), 1.0) for z in range(layers)]
        between = jnp.where(inside, flow(perm[0], perm[1]), 0.0)
        faces, scale = [], []
        for z in range(layers):
            below = jnp.where(joined, flow(perm[z], row_next(perm[z])), 0.0)
            right = jnp.where(not_last, flow(perm[z], col_next(perm[z])), 0.0)
            right = jnp.where(inside, right, 0.0)
            face = (below, row_prev(below), right, col_prev(right))
            faces.append(face)
            scale.append(1.0 / (1.0 + between + face[0] + face[1] + face[2] + face[3]))
        press, near = start, around
        for turn in range(SWEEPS):
            if turn > 0:
                near = [[f(press[z]) for f in (row_next, row_prev, col_next, col_prev)] for z in range(layers)]
            press = [
                (base[z] + between * press[1 - z] + sum(c * v for c, v in zip(faces[z], near[z]))) * scale[z]
                for z in range(layers)
            ]
        cols = width // parts
        for z in range(layers):
            press_scr[...] = press[z][:rows]
            for k in range(parts):
                at = pl.multiple_of(target(mem, k, parts) * cols, cols)
                press_refs[k][member, z] = press_scr[:, pl.ds(at, cols)]
            weight = perm[z][:rows]
            for kind, value in enumerate((weight * press[z][:rows], weight)):
                hi = value.astype(BF)
                lo = (value - hi.astype(F32)).astype(BF)
                for part, piece in enumerate((hi, lo)):
                    at = (((kind * 2 + part) * members + member) * layers + z) * rows
                    v_scr[pl.ds(pl.multiple_of(at, rows), rows), :] = piece
        return 0

    lax.fori_loop(0, members, sweep, 0)

    slots, wells = ids_ref.shape
    cells = layers * rows
    layer_at, rest = split(ids_ref[...], grid_rows * width)
    row_at, col = split(rest, width)
    row_at = row_at - tile * rows
    used = (iota((slots, wells), 0) < count_ref[...]) & (row_at >= 0) & (row_at < rows)
    sel = jnp.where(used, layer_at * rows + row_at, -1)
    sums = jnp.zeros((4 * members, wells), F32)
    for slot in range(0, slots, 2):
        sel_two = jnp.concatenate([sel[slot : slot + 1], sel[slot + 1 : slot + 2]], axis=1)
        col_two = jnp.concatenate([col[slot : slot + 1], col[slot + 1 : slot + 2]], axis=1)
        here = iota((width, 2 * wells), 0) == col_two
        got = jnp.dot(v_scr[...], jnp.where(here, 1.0, 0.0).astype(BF), preferred_element_type=F32)
        mine = iota((cells, 2 * wells), 0) == sel_two
        picked = jnp.where(mine[None], got.reshape(4 * members, cells, 2 * wells), 0.0)
        both = jnp.sum(picked, axis=1)
        sums = sums + both[:, :wells] + both[:, wells:]
    sums_ref[0:members] = sums[0:members] + sums[members : 2 * members]
    sums_ref[members : 2 * members] = sums[2 * members : 3 * members] + sums[3 * members :]


def decode(parts, tile_vec, mem_vec, grid_rows, field, near, far, prev, src, win, wmix, gains, ids, counts):
    layers, members, rows, width = field.shape
    groups = layers * members
    total = groups * width // 2
    wells = ids.shape[1]
    return pl.pallas_call(
        functools.partial(decode_kernel, grid_rows),
        in_specs=[SMEM] * 2 + [VMEM] * 10,
        out_specs=[VMEM] * (parts + 1),
        out_shape=[jax.ShapeDtypeStruct((members, layers, rows, width // parts), F32)] * parts
        + [jax.ShapeDtypeStruct((2 * members, wells), F32)],
        scratch_shapes=[
            pltpu.VMEM((groups, RING, width), F32),
            pltpu.VMEM((groups // 2, width + 8, 128), F32),
            pltpu.VMEM((total, 256), BF),
            pltpu.VMEM((HELD + 1, total, 256), BF),
            pltpu.VMEM((HELD + 1, total, 256), BF),
            pltpu.VMEM((MIX_BLOCKS, total, 128), BF),
            pltpu.VMEM((MIX_BLOCKS * 128, 128), BF),
            pltpu.VMEM((4 * groups * rows, width), BF),
            pltpu.VMEM((rows, width), F32),
            pltpu.VMEM((groups + 2 * layers, 8, width), F32),
        ],
        compiler_params=pltpu.CompilerParams(vmem_limit_bytes=40 * 2**20),
    )(tile_vec, mem_vec, field, near, far, prev, src, win, wmix, gains, ids, counts)


def update_kernel(mem_ref, refs, swap_refs, obs_ref, err_ref, press_ref, data_ref, new_ref, all_scr, step_scr):
    count = len(refs)
    own = refs[0].shape[0]
    members, wells = obs_ref.shape
    mem = mem_ref[0]
    for k in range(count):
        source = origin(mem, k, count)
        all_scr[source] = refs[k][...]
        press_ref[source] = swap_refs[k][...]
    every = jnp.concatenate([all_scr[k] for k in range(count)], axis=0)
    data, every = every[:, :wells], every[:, wells:]
    data_ref[...] = data
    scale = 2.0 * err_ref[...]
    root = math.sqrt(members - 1)
    scaled = (data - jnp.mean(data, axis=0, keepdims=True)) / (root * scale)
    innov = (obs_ref[...] - data) / scale
    dims = (((1,), (1,)), ((), ()))
    exact = lax.Precision.HIGHEST
    eye = (iota((members, members), 0) == iota((members, members), 1)).astype(F32)
    gram = eye + lax.dot_general(scaled, scaled, dims, precision=exact, preferred_element_type=F32)
    cross = lax.dot_general(innov, scaled, dims, precision=exact, preferred_element_type=F32)
    right = (every - jnp.mean(every, axis=0, keepdims=True)) / root
    place = iota((members, 128), 0)
    places = iota(right.shape, 0)
    cols = [jnp.broadcast_to(gram[:, k : k + 1], (members, 128)) for k in range(members)]
    for k in range(members):
        inverse = 1.0 / cols[k][k : k + 1]
        factor = jnp.where(place == k, 0.0, cols[k])
        for i in range(k + 1, members):
            row = cols[i][k : k + 1] * inverse
            cols[i] = jnp.where(place == k, row, cols[i] - factor * row)
        row = right[k : k + 1] * jnp.concatenate([inverse] * (right.shape[1] // 128), axis=1)
        wide = jnp.concatenate([factor] * (right.shape[1] // 128), axis=1)
        right = jnp.where(places == k, row, right - wide * row)
    new = every + jnp.dot(cross, right, precision=exact, preferred_element_type=F32)
    for k in range(count):
        step_scr[k] = new[k * own : (k + 1) * own]
    new_ref[...] = step_scr[mem]


def update(mem_vec, pieces, swaps, obs, err):
    count = len(pieces)
    own, total = pieces[0].shape
    members, wells = obs.shape

    def kernel(mem_ref, *refs):
        update_kernel(mem_ref, refs[:count], refs[count : 2 * count], *refs[2 * count :])

    return pl.pallas_call(
        kernel,
        in_specs=[SMEM] + [VMEM] * (2 * count + 2),
        out_specs=[VMEM] * 3,
        out_shape=[
            jax.ShapeDtypeStruct((count,) + swaps[0].shape, F32),
            jax.ShapeDtypeStruct((members, wells), F32),
            jax.ShapeDtypeStruct((own, total - wells), F32),
        ],
        scratch_shapes=[
            pltpu.VMEM((count, own, total), F32),
            pltpu.VMEM((count, own, total - wells), F32),
        ],
        compiler_params=pltpu.CompilerParams(vmem_limit_bytes=24 * 2**20),
    )(mem_vec, *pieces, *swaps, obs, err)


def gathered(pieces, axis):
    count = lax.axis_size(axis)
    return [pieces[0]] + [
        lax.ppermute(pieces[k], axis, [(i, target(i, k, count)) for i in range(count)]) for k in range(1, count)
    ]


def summed(own, axis):
    count = lax.axis_size(axis)
    if count & (count - 1):
        return lax.psum(own, axis)
    k = 1
    while k < count:
        jumps = (k, 2 * k, 3 * k) if 4 * k <= count else (k,)
        own = own + sum(lax.ppermute(own, axis, [(i, i ^ j) for i in range(count)]) for j in jumps)
        k *= len(jumps) + 1
    return own


def halo(near, far, axis):
    count = lax.axis_size(axis)
    swap = lambda first: [p for i in range(first, count - 1, 2) for p in ((i, i + 1), (i + 1, i))]
    far = lax.ppermute(far, axis, swap(1))
    return lax.ppermute(near, axis, swap(0)), far


def body(
    latents,
    basis,
    conv_in,
    conv_mid,
    conv_out,
    pressure_prev,
    source,
    perf_cells,
    perf_count,
    obs_perturbed,
    obs_error,
):
    members = latents.shape[0]
    layers, rows, width = basis.shape[1:]
    tiles = lax.axis_size("tile")
    parts = lax.axis_size("mem")
    grid_rows = rows * tiles
    tile_vec = lax.axis_index("tile").astype(jnp.int32).reshape(1)
    mem_vec = lax.axis_index("mem").astype(jnp.int32).reshape(1)

    field, near, far = field_of(tile_vec, latents, basis, pressure_prev, source)
    near, far = halo(near, far, "tile")
    win, wmix, gains = placed(tile_vec, grid_rows, rows, conv_in, conv_mid, conv_out.reshape(1, -1))
    *press, sums = decode(
        parts, tile_vec, mem_vec, grid_rows, field, near, far, pressure_prev, source,
        win, wmix, gains, perf_cells.T, perf_count.reshape(1, -1),
    )
    swaps = gathered(press, "mem")
    sums = summed(sums, "tile")
    well = jnp.concatenate([sums[:members] / sums[members:], latents], axis=1)
    pieces = gathered([well] * parts, "mem")
    press, data, new = update(mem_vec, pieces, swaps, obs_perturbed, obs_error.reshape(1, -1))
    return (press.reshape((parts * members,) + press.shape[2:]), data, new)


def solution(mesh):
    return jax.shard_map(
        body,
        mesh=mesh,
        in_specs=(
            P("mem", None),
            P(None, None, "tile", None),
            P(),
            P(),
            P(),
            P(None, "tile", None),
            P(None, "tile", None),
            P(),
            P(),
            P(),
            P(),
        ),
        out_specs=(P(None, None, "tile", "mem"), P(), P("mem", None)),
        check_vma=False,
    )
```

```python
import functools
import math

import jax
import jax.numpy as jnp
from jax import lax
from jax.experimental import pallas as pl
from jax.experimental.pallas import tpu as pltpu
from jax.sharding import PartitionSpec as P

SWEEPS = 2
PACKED = 96
HALO = 4
RING = 24
LIFT_BLOCKS = 11
INNER = (3, 8)
FIRST = ((4, 0), (5, 1), (6, 2))
ORDER = ((5, 7, 3), (6, 3, 4), (4, 8, 5), (7, 2, 1), (3, 9, 2), (8, 1, 0), (2, 10, 3), (9, 0, 4), (1, None, None), (10, None, None))
MIX_BLOCKS = 10
SEG = 16
BF = jnp.bfloat16
F32 = jnp.float32
VMEM = pl.BlockSpec(memory_space=pltpu.VMEM)
SMEM = pl.BlockSpec(memory_space=pltpu.SMEM)


def iota(shape, dim):
    return lax.broadcasted_iota(jnp.int32, shape, dim)


def place_weights(tile, grid_rows, rows, in_ref, mid_ref, out_ref, win_ref, wmix_ref, gain_ref):
    one = lambda mask: jnp.where(mask, 1.0, 0.0).astype(BF)
    dot = functools.partial(jnp.dot, preferred_element_type=F32)
    taps = dot(one(iota((64, 9), 0) & 15 == iota((64, 9), 1)), in_ref[...]).astype(BF)
    taps = dot(taps, one(iota((64, 256), 0) == iota((64, 256), 1) & 63))
    kinds = jnp.where(iota((64, 256), 0) >> 4 == iota((64, 256), 1) >> 6, taps, 0.0).astype(BF)
    k, j = iota((256, 64), 0), iota((256, 64), 1)
    lane = k & 127
    own = lane < 64
    offset = 2 * (k >> 7) + jnp.where(own, lane >> 5, ((lane - 64) >> 4) & 1)
    ring = jnp.where(own, lane & 15, jnp.where(lane < 96, 16 + (lane & 7), 2 * RING))
    place, tap = j >> 4, j & 15
    xx, yy = place >> 1, place & 1
    a = ((tap * 11) >> 5) - 1
    b = tap - 3 * (a + 1) - 1
    fits = (tap < 9) & (offset == yy + b + 1)
    for block in range(LIFT_BLOCKS):
        row = jnp.where(xx == 0, 18, -3) if block == 0 else 2 * block - HALO + xx
        near = row + a
        near = jnp.where(near < 0, near + RING, near)
        grid_row = tile * rows + row
        pick = fits & (ring == near) & (grid_row >= 0) & (grid_row < grid_rows)
        win_ref[block] = dot(one(pick), kinds).astype(BF)
    o, n = iota((64, 1024), 0), iota((64, 1024), 1)
    put = one(n & 255 == (o >> 5) * 128 + (n >> 8) * 32 + (o & 31))
    placed = [
        lax.dot_general(mid_ref[t], put, (((0,), (0,)), ((), ())), preferred_element_type=F32) for t in range(9)
    ]
    for kind in range(4):
        side, over = kind & 1, kind >> 1
        for place_in in range(4):
            xi, yi = place_in >> 1, place_in & 1
            total = jnp.zeros((64, 256), F32)
            for place_out in range(4):
                xo, yo = place_out >> 1, place_out & 1
                dx = xi - xo + (0 if not over else (2 if xi == 0 else -2))
                dy = yi - yo + (0 if not side else (2 if yi == 0 else -2))
                if abs(dx) <= 1 and abs(dy) <= 1:
                    t = 3 * (dx + 1) + dy + 1
                    total = total + placed[t][:, 256 * place_out : 256 * place_out + 256]
            at = 256 * kind + 64 * place_in
            wmix_ref[at : at + 64, :] = total.astype(BF)
    gains = jnp.broadcast_to(out_ref[...].astype(F32), (8, 64)).astype(BF)
    c, n = iota((64, 128), 0), iota((64, 128), 1)
    gain_ref[0:8] = dot(gains, one(c == n & 31))
    gain_ref[8:16] = dot(gains, one(c == 32 + (n & 31)))


def shifted(f):
    hi = f.astype(BF).astype(F32)
    lo = f - hi
    edge = iota(f.shape, 1) == 0
    return [jnp.where(edge, 0.0, pltpu.roll(v, 1, 1)) for v in (hi, lo)] + [hi, lo]


def turned(parts, span, scr):
    width = parts[0].shape[1]
    tall = jnp.concatenate(parts, axis=0).T
    scr[0:width, :] = tall
    end = pltpu.roll(tall[width - 8 : width], 128 - span // 2, 1)
    end = jnp.where(iota(end.shape, 1) & (span - 1) < span // 2, end, 0.0)
    scr[width : width + 8, :] = pltpu.roll(end, 1, 0)


def lift_block(pt, win, put_lift, put_side):
    total = pt.shape[0]
    wide = jnp.maximum(jnp.dot(pt, win, preferred_element_type=F32), 0.0)
    put_lift(wide.astype(BF))
    right = iota((SEG, 256), 1) & 64 == 0
    row = iota((SEG, 256), 0)
    steps = SEG
    for base in range(0, total, steps * SEG):
        last = base + (steps - 1) * SEG
        after = jnp.where(row < SEG - 1, pltpu.roll(wide[base : base + SEG], SEG - 1, 0), 0.0)
        before = jnp.where(row > 0, pltpu.roll(wide[last : last + SEG], 1, 0), 0.0)
        for q in range(steps):
            r = base + q * SEG
            nxt = after if q == steps - 1 else wide[r + SEG : r + 2 * SEG]
            prv = before if q == 0 else wide[r - SEG : r]
            put_side(r, jnp.where(right, nxt, prv).astype(BF))


def lift_to(pt_ref, win, lift_ref, side_ref, slot):
    def put_lift(v):
        lift_ref[slot] = v

    def put_side(r, v):
        side_ref[slot, r : r + SEG, :] = v

    lift_block(pt_ref[...], win, put_lift, put_side)


def early_kernel(
    grid_rows,
    tile_ref,
    field_hbm,
    in_ref,
    mid_ref,
    out_ref,
    field_ref,
    win_ref,
    wmix_ref,
    gain_ref,
    pt_ref,
    t_scr,
    sem,
):
    layers, members, rows, width = field_ref.shape
    groups = layers * members
    steps = width // (2 * SEG)
    block_rows = width // 2
    copy = pltpu.make_async_copy(field_hbm, field_ref, sem)
    copy.start()
    place_weights(tile_ref[0], grid_rows, rows, in_ref, mid_ref, out_ref, win_ref, wmix_ref, gain_ref)
    copy.wait()

    def load(pair, _):
        parts = []
        for half in range(2):
            group = 2 * pair + half
            parts += shifted(field_ref[group // members, lax.rem(group, members)])
        turned(parts, 4 * rows, t_scr)
        mine = iota((SEG, 128), 1) < 4 * rows
        for q in range(steps + 1):
            part = t_scr[pl.ds(2 * q, SEG, stride=2 * steps), :]
            for half in range(2):
                v = jnp.where(mine, part if half == 0 else pltpu.roll(part, 64, 1), 0.0).astype(BF)
                at = (2 * pair + half) * block_rows + q * SEG
                if q < steps:
                    pt_ref[pl.ds(pl.multiple_of(at, SEG), SEG), 0:128] = v
                if q > 0:
                    pt_ref[pl.ds(pl.multiple_of(at - SEG, SEG), SEG), 128:256] = v
        return 0

    lax.fori_loop(0, groups // 2, load, 0)


def early(tile_vec, grid_rows, field, conv_in, conv_mid, conv_out):
    layers, members, rows, width = field.shape
    total = layers * members * width // 2
    return pl.pallas_call(
        functools.partial(early_kernel, grid_rows),
        in_specs=[SMEM, pl.BlockSpec(memory_space=pltpu.HBM)] + [VMEM] * 3,
        out_specs=[VMEM] * 5,
        out_shape=[
            jax.ShapeDtypeStruct(field.shape, F32),
            jax.ShapeDtypeStruct((LIFT_BLOCKS, 256, 256), BF),
            jax.ShapeDtypeStruct((1024, 256), BF),
            jax.ShapeDtypeStruct((16, 128), F32),
            jax.ShapeDtypeStruct((total, 256), BF),
        ],
        scratch_shapes=[pltpu.VMEM((width + 8, 128), F32), pltpu.SemaphoreType.DMA],
        compiler_params=pltpu.CompilerParams(vmem_limit_bytes=16 * 2**20),
        cost_estimate=pl.CostEstimate(flops=900_000_000, bytes_accessed=3_000_000, transcendentals=0),
    )(tile_vec, field, conv_in, conv_mid, conv_out)


def field_kernel(tile_ref, lat_hbm, basis_ref, prev_hbm, src_hbm, field_ref, near_ref, far_ref, held, lat_ref, prev_ref, src_ref, sems):
    chunks, comps, layers, rows, width = held.shape
    members, total = lat_ref.shape
    span = comps * rows
    copies = [
        pltpu.make_async_copy(basis_ref.at[pl.ds(c * comps, comps)], held.at[c], sems.at[c]) for c in range(chunks)
    ]
    small = [
        pltpu.make_async_copy(a, b, sems.at[chunks + i])
        for i, (a, b) in enumerate(((lat_hbm, lat_ref), (prev_hbm, prev_ref), (src_hbm, src_ref)))
    ]
    for copy in small[:1] + copies + small[1:]:
        copy.start()
    even_tile = tile_ref[0] & 1 == 0
    shape = (PACKED, 2 * (layers * members + 2 * layers) * rows)
    picks = [packed_from(layers, members, rows, up, shape) for up in (even_tile, jnp.logical_not(even_tile))]
    small[0].wait()
    lat = lat_ref[...].astype(BF)
    own = iota((rows, span), 0) == iota((rows, span), 1) & (rows - 1)
    behind = iota((total, span), 0) - split(iota((total, span), 1), rows)[0]
    for c in range(chunks):
        pick = jnp.where(behind == c * comps, 1.0, 0.0).astype(BF)
        spread = jnp.dot(lat, pick, preferred_element_type=F32)
        left = jnp.where(own[None], spread[:, None, :], 0.0).astype(BF).reshape(members * rows, span)
        copies[c].wait()
        for z in range(layers):
            part = jnp.dot(left, held[c, :, z].reshape(span, width), preferred_element_type=F32)
            part = part.reshape(members, rows, width)
            field_ref[z] = part if c == 0 else field_ref[z] + part
    small[1].wait()
    small[2].wait()
    exact, rest = [], []
    for value in (field_ref[...].reshape(-1, width), prev_ref[...].reshape(-1, width), src_ref[...].reshape(-1, width)):
        hi = value.astype(BF)
        exact.append(hi)
        rest.append((value - hi.astype(F32)).astype(BF))
    pool = jnp.concatenate([exact[0], rest[0], exact[1], rest[1], exact[2], rest[2]], axis=0)
    for ref, pick in zip((near_ref, far_ref), picks):
        ref[...] = jnp.dot(pick, pool, preferred_element_type=F32).astype(BF)


def packed_from(layers, members, rows, upper, shape):
    groups = layers * members
    r, at = iota((shape[0], 1), 0), iota(shape, 1)
    last = jnp.where(upper, 1, 0)
    group = (r * 43) >> 8
    j = r - 6 * group
    row_hi = jnp.where(last == 1, rows - HALO + j, j)
    row_lo = jnp.where(last == 1, rows - 2 + j - HALO, j - HALO)
    field = jnp.where(j < HALO, group * rows + row_hi, (groups + group) * rows + row_lo)
    p = r - 6 * groups
    half, j = (p >> 1) & 1, p & 1
    prev = (2 * groups + half * layers + (p >> 2)) * rows + jnp.where(last == 1, rows - 2 + j, j)
    s = p - 4 * layers
    src = (2 * groups + (2 + (s & 1)) * layers + (s >> 1)) * rows + jnp.where(last == 1, rows - 1, 0)
    wanted = jnp.where(p < 0, field, jnp.where(s < 0, prev, jnp.where(s < 2 * layers, src, -1)))
    return jnp.where(wanted == at, 1.0, 0.0).astype(BF)


def unpacked_to(layers, members, upper, shape):
    groups = layers * members
    r, at = iota((shape[0], 1), 0), iota(shape, 1)
    group, s = r >> 3, r & 7
    up = jnp.where(upper, 1, 0)
    j = jnp.where(up == 1, s - HALO, s)
    mine = (j >= 0) & (j < HALO)
    near = jnp.where(up == 1, j - 2, j)
    close = mine & (near >= 0) & (near < 2)
    z = group - groups
    hi = jnp.where(z < 0, group * 6 + j, 6 * groups + z * 4 + near)
    lo = jnp.where(z < 0, group * 6 + HALO + near, 6 * groups + z * 4 + 2 + near)
    is_src = z >= layers
    src = 6 * groups + 4 * layers + 2 * (z - layers)
    edge = close & (jnp.where(up == 1, near, 1 - near) == 1)
    hi = jnp.where(is_src, src, hi)
    lo = jnp.where(is_src, src + 1, lo)
    use_hi = (z < 0) & mine | (z >= 0) & (z < layers) & close | is_src & edge
    use_lo = (z < layers) & close | is_src & edge
    return jnp.where(use_hi & (at == hi) | use_lo & (at == lo), 1.0, 0.0).astype(BF)


def field_of(tile_vec, latents, basis, prev, src):
    total, layers, rows, width = basis.shape
    members = latents.shape[0]
    comps = 32
    return pl.pallas_call(
        field_kernel,
        in_specs=[SMEM] + [pl.BlockSpec(memory_space=pltpu.HBM)] * 4,
        out_specs=[VMEM] * 3,
        out_shape=[
            jax.ShapeDtypeStruct((layers, members, rows, width), F32),
            jax.ShapeDtypeStruct((PACKED, width), BF),
            jax.ShapeDtypeStruct((PACKED, width), BF),
        ],
        scratch_shapes=[
            pltpu.VMEM((total // comps, comps, layers, rows, width), BF),
            pltpu.VMEM(latents.shape, F32),
            pltpu.VMEM(prev.shape, F32),
            pltpu.VMEM(src.shape, F32),
            pltpu.SemaphoreType.DMA((total // comps + 3,)),
        ],
        compiler_params=pltpu.CompilerParams(vmem_limit_bytes=57 * 2**20),
    )(tile_vec, latents, basis, prev, src)


def target(me, k, count):
    return (me + k) % count if count & (count - 1) else me ^ k


def origin(me, k, count):
    return (me + count - k) % count if count & (count - 1) else me ^ k


def split(value, by):
    if by & (by - 1):
        return value // by, value % by
    return value >> (by.bit_length() - 1), value & (by - 1)


def decode_kernel(
    grid_rows,
    tile_ref,
    mem_ref,
    field_ref,
    near_ref,
    far_ref,
    prev_ref,
    src_ref,
    win_ref,
    wmix_ref,
    gain_ref,
    early_pt_ref,
    ids_ref,
    count_ref,
    *refs,

):
    parts = len(refs) - 11
    press_refs, sums_ref = refs[:parts], refs[parts]
    f_scr, t_scr, pt_scr, lift_scr, side_scr, deep_scr, wout_scr, v_scr, press_scr, third_scr = refs[parts + 1 :]
    layers, members, rows, width = field_ref.shape
    groups = layers * members
    steps = width // (2 * SEG)
    block_rows = width // 2
    tile, mem = tile_ref[0], mem_ref[0]
    even_tile = tile & 1 == 0

    shape = ((groups + 2 * layers) * 8, PACKED)
    from_near = unpacked_to(layers, members, jnp.logical_not(even_tile), shape)
    from_far = unpacked_to(layers, members, even_tile, shape)
    third_scr[...] = (
        jnp.dot(from_near, near_ref[...], preferred_element_type=F32)
        + jnp.dot(from_far, far_ref[...], preferred_element_type=F32)
    ).reshape(-1, 8, width)

    def load(quad):
        parts = []
        for j in range(4):
            parts += shifted(third_scr[4 * quad + j])
        turned(parts, 32, t_scr.at[quad])
        lane = iota((SEG, 128), 1)
        mine = (lane >= 64) & (lane < 96)
        for q in range(steps + 1):
            part = t_scr[quad, pl.ds(2 * q, SEG, stride=2 * steps), :]
            for j in range(4):
                v = part if j == 2 else pltpu.roll(part, (64 - 32 * j) % 128, 1)
                v = jnp.where(mine, v, 0.0).astype(BF)
                at = (4 * quad + j) * block_rows + q * SEG
                if q < steps:
                    rows_at = pl.ds(pl.multiple_of(at, SEG), SEG)
                    pt_scr[rows_at, 0:128] = early_pt_ref[rows_at, 0:128] + v
                if q > 0:
                    rows_at = pl.ds(pl.multiple_of(at - SEG, SEG), SEG)
                    pt_scr[rows_at, 128:256] = early_pt_ref[rows_at, 128:256] + v

    gain0, gain1 = gain_ref[0:1, :], gain_ref[8:9, :]

    places = {}

    begun = set()

    def mix(block, here, above, below):
        x = jnp.concatenate(
            [
                here[0][here[2]],
                here[1][here[2]],
                below[0][below[2], :, 0:128],
                above[0][above[2], :, 128:256],
                below[1][below[2], :, 0:128],
                above[1][above[2], :, 128:256],
            ],
            axis=1,
        )
        deep = jnp.maximum(jnp.dot(x, wmix_ref[...], preferred_element_type=F32), 0.0)
        deep = deep[:, :128] * gain0 + deep[:, 128:] * gain1
        place, part = divmod(block - 1, 4)
        deep = deep + pltpu.roll(deep, 16 if part & 2 else 112, 1)
        deep = deep + pltpu.roll(deep, 8 if part & 1 else 120, 1)
        deep = jnp.where((iota(deep.shape, 1) & 31) >> 3 == part, deep, 0.0).astype(BF)
        deep_scr[place] = deep if place not in begun else deep_scr[place] + deep
        begun.add(place)

    def lift(block, slot):
        lift_to(early_pt_ref if INNER[0] <= block <= INNER[1] else pt_scr, win_ref[block], lift_scr, side_scr, slot)
        places[block] = (lift_scr, side_scr, slot)

    for block, slot in FIRST:
        lift(block, slot)
    for step, (block, lifted, slot) in enumerate(ORDER):
        mix(block, places[block], places[block - 1], places[(block + 1) % LIFT_BLOCKS])
        if step < groups // 4:
            load(step)
        if lifted is not None:
            lift(lifted, slot)

    k, n = iota(wout_scr.shape, 0), iota(wout_scr.shape, 1)
    place = (k & 127) >> 5
    row = 2 * (4 * (k >> 7) + ((k & 31) >> 3) + 1) - HALO + (place >> 1)
    row = jnp.where(row < 0, row + RING, row)
    wout_scr[...] = jnp.where(n == (place & 1) * 32 + row, 1.0, 0.0).astype(BF)

    def collect(pair, held):
        at = pl.ds(pl.multiple_of(pair * 2 * block_rows, 2 * block_rows), 2 * block_rows)
        x = jnp.concatenate([deep_scr[j, at, :] for j in range(deep_scr.shape[0])], axis=1)
        both = jnp.dot(x, wout_scr[...], preferred_element_type=F32)
        both = both[:block_rows] + pltpu.roll(both[block_rows:], 64, 1)
        for q in range(steps):
            part = both[q * SEG : (q + 1) * SEG]
            t_scr[held, pl.ds(2 * q, SEG, stride=2 * steps), :] = part
            t_scr[held, pl.ds(2 * q + 1, SEG, stride=2 * steps), :] = part
        flat = t_scr[held, 0:width, :].T
        even = iota((RING, width), 1) & 1 == 0
        for half in range(2):
            s = 64 * half
            group = 2 * pair + half
            f = jnp.concatenate([field_ref[group // members, group % members], third_scr[group]], axis=0)
            f_scr[group] = f + jnp.where(
                even, flat[s : s + RING], flat[s + 32 : s + 32 + RING]
            )

    for pair in range(groups // 2):
        collect(pair, pair % (groups // 4))

    full = (RING, width)
    ring = iota(full, 0)
    grid_row = tile * rows + jnp.where(ring < rows + HALO, ring, ring - RING)
    inside = (grid_row >= 0) & (grid_row < grid_rows)
    joined = (grid_row >= 0) & (grid_row < grid_rows - 1)
    not_last = iota(full, 1) < width - 1

    def ring_of(ref, group, z):
        return jnp.concatenate([ref[z], third_scr[group]], axis=0)

    def row_next(v):
        return pltpu.roll(v, RING - 1, 0)

    def row_prev(v):
        return pltpu.roll(v, 1, 0)

    def col_next(v):
        return pltpu.roll(v, width - 1, 1)

    def col_prev(v):
        return pltpu.roll(v, 1, 1)

    start = [ring_of(prev_ref, groups + z, z) for z in range(layers)]
    base = [start[z] + ring_of(src_ref, groups + layers + z, z) for z in range(layers)]
    around = [[f(start[z]) for f in (row_next, row_prev, col_next, col_prev)] for z in range(layers)]

    def flow(p, q):
        return 2.0 * p * q / (p + q)

    def sweep(member, _):
        perm = [jnp.where(inside, jnp.exp(f_scr[z * members + member]), 1.0) for z in range(layers)]
        between = jnp.where(inside, flow(perm[0], perm[1]), 0.0)
        faces, scale = [], []
        for z in range(layers):
            below = jnp.where(joined, flow(perm[z], row_next(perm[z])), 0.0)
            right = jnp.where(not_last, flow(perm[z], col_next(perm[z])), 0.0)
            right = jnp.where(inside, right, 0.0)
            face = (below, row_prev(below), right, col_prev(right))
            faces.append(face)
            scale.append(1.0 / (1.0 + between + face[0] + face[1] + face[2] + face[3]))
        press, near = start, around
        for turn in range(SWEEPS):
            if turn > 0:
                near = [[f(press[z]) for f in (row_next, row_prev, col_next, col_prev)] for z in range(layers)]
            press = [
                (base[z] + between * press[1 - z] + sum(c * v for c, v in zip(faces[z], near[z]))) * scale[z]
                for z in range(layers)
            ]
        cols = width // parts
        for z in range(layers):
            press_scr[...] = press[z][:rows]
            for k in range(parts):
                at = pl.multiple_of(target(mem, k, parts) * cols, cols)
                press_refs[k][member, z] = press_scr[:, pl.ds(at, cols)]
            weight = perm[z][:rows]
            for kind, value in enumerate((weight * press[z][:rows], weight)):
                hi = value.astype(BF)
                lo = (value - hi.astype(F32)).astype(BF)
                for part, piece in enumerate((hi, lo)):
                    at = (((kind * 2 + part) * members + member) * layers + z) * rows
                    v_scr[pl.ds(pl.multiple_of(at, rows), rows), :] = piece
        return 0

    lax.fori_loop(0, members, sweep, 0)

    slots, wells = ids_ref.shape
    cells = layers * rows
    layer_at, rest = split(ids_ref[...], grid_rows * width)
    row_at, col = split(rest, width)
    row_at = row_at - tile * rows
    used = (iota((slots, wells), 0) < count_ref[...]) & (row_at >= 0) & (row_at < rows)
    sel = jnp.where(used, layer_at * rows + row_at, -1)
    sums = jnp.zeros((4 * members, wells), F32)
    for slot in range(0, slots, 2):
        sel_two = jnp.concatenate([sel[slot : slot + 1], sel[slot + 1 : slot + 2]], axis=1)
        col_two = jnp.concatenate([col[slot : slot + 1], col[slot + 1 : slot + 2]], axis=1)
        here = iota((width, 2 * wells), 0) == col_two
        got = jnp.dot(v_scr[...], jnp.where(here, 1.0, 0.0).astype(BF), preferred_element_type=F32)
        mine = iota((cells, 2 * wells), 0) == sel_two
        picked = jnp.where(mine[None], got.reshape(4 * members, cells, 2 * wells), 0.0)
        both = jnp.sum(picked, axis=1)
        sums = sums + both[:, :wells] + both[:, wells:]
    sums_ref[0:members] = sums[0:members] + sums[members : 2 * members]
    sums_ref[members : 2 * members] = sums[2 * members : 3 * members] + sums[3 * members :]


def decode(parts, tile_vec, mem_vec, grid_rows, field, near, far, prev, src, weights, ids, counts):
    layers, members, rows, width = field.shape
    groups = layers * members
    total = groups * width // 2
    wells = ids.shape[1]
    return pl.pallas_call(
        functools.partial(decode_kernel, grid_rows),
        in_specs=[SMEM] * 2 + [VMEM] * 11,
        out_specs=[VMEM] * (parts + 1),
        out_shape=[jax.ShapeDtypeStruct((members, layers, rows, width // parts), F32)] * parts
        + [jax.ShapeDtypeStruct((2 * members, wells), F32)],
        scratch_shapes=[
            pltpu.VMEM((groups, RING, width), F32),
            pltpu.VMEM((groups // 4, width + 8, 128), F32),
            pltpu.VMEM((total, 256), BF),
            pltpu.VMEM((1 + max(o[2] for o in ORDER if o[2] is not None), total, 256), BF),
            pltpu.VMEM((1 + max(o[2] for o in ORDER if o[2] is not None), total, 256), BF),
            pltpu.VMEM((-(-MIX_BLOCKS // 4), total, 128), BF),
            pltpu.VMEM((-(-MIX_BLOCKS // 4) * 128, 128), BF),
            pltpu.VMEM((4 * groups * rows, width), BF),
            pltpu.VMEM((rows, width), F32),
            pltpu.VMEM((groups + 2 * layers, 8, width), F32),
        ],
        compiler_params=pltpu.CompilerParams(vmem_limit_bytes=43 * 2**20),
    )(tile_vec, mem_vec, field, near, far, prev, src, *weights, ids, counts)


def update_kernel(mem_ref, refs, swap_refs, obs_ref, err_ref, press_ref, data_ref, new_ref, all_scr, step_scr):
    count = len(refs)
    own = refs[0].shape[0]
    members, wells = obs_ref.shape
    mem = mem_ref[0]
    for k in range(count):
        source = origin(mem, k, count)
        all_scr[source] = refs[k][...]
        press_ref[source] = swap_refs[k][...]
    every = jnp.concatenate([all_scr[k] for k in range(count)], axis=0)
    data, every = every[:, :wells], every[:, wells:]
    data_ref[...] = data
    scale = 2.0 * err_ref[...]
    root = math.sqrt(members - 1)
    scaled = (data - jnp.mean(data, axis=0, keepdims=True)) / (root * scale)
    innov = (obs_ref[...] - data) / scale
    dims = (((1,), (1,)), ((), ()))
    exact = lax.Precision.HIGHEST
    eye = (iota((members, members), 0) == iota((members, members), 1)).astype(F32)
    gram = eye + lax.dot_general(scaled, scaled, dims, precision=exact, preferred_element_type=F32)
    cross = lax.dot_general(innov, scaled, dims, precision=exact, preferred_element_type=F32)
    right = (every - jnp.mean(every, axis=0, keepdims=True)) / root
    place = iota((members, 128), 0)
    places = iota(right.shape, 0)
    cols = [jnp.broadcast_to(gram[:, k : k + 1], (members, 128)) for k in range(members)]
    for k in range(members):
        inverse = 1.0 / cols[k][k : k + 1]
        factor = jnp.where(place == k, 0.0, cols[k])
        for i in range(k + 1, members):
            row = cols[i][k : k + 1] * inverse
            cols[i] = jnp.where(place == k, row, cols[i] - factor * row)
        row = right[k : k + 1] * jnp.concatenate([inverse] * (right.shape[1] // 128), axis=1)
        wide = jnp.concatenate([factor] * (right.shape[1] // 128), axis=1)
        right = jnp.where(places == k, row, right - wide * row)
    new = every + jnp.dot(cross, right, precision=exact, preferred_element_type=F32)
    for k in range(count):
        step_scr[k] = new[k * own : (k + 1) * own]
    new_ref[...] = step_scr[mem]


def update(mem_vec, pieces, swaps, obs, err):
    count = len(pieces)
    own, total = pieces[0].shape
    members, wells = obs.shape

    def kernel(mem_ref, *refs):
        update_kernel(mem_ref, refs[:count], refs[count : 2 * count], *refs[2 * count :])

    return pl.pallas_call(
        kernel,
        in_specs=[SMEM] + [VMEM] * (2 * count + 2),
        out_specs=[VMEM] * 3,
        out_shape=[
            jax.ShapeDtypeStruct((count,) + swaps[0].shape, F32),
            jax.ShapeDtypeStruct((members, wells), F32),
            jax.ShapeDtypeStruct((own, total - wells), F32),
        ],
        scratch_shapes=[
            pltpu.VMEM((count, own, total), F32),
            pltpu.VMEM((count, own, total - wells), F32),
        ],
        compiler_params=pltpu.CompilerParams(vmem_limit_bytes=24 * 2**20),
    )(mem_vec, *pieces, *swaps, obs, err)


def gathered(pieces, axis):
    count = lax.axis_size(axis)
    return [pieces[0]] + [
        lax.ppermute(pieces[k], axis, [(i, target(i, k, count)) for i in range(count)]) for k in range(1, count)
    ]


def summed(own, axis):
    count = lax.axis_size(axis)
    if count & (count - 1):
        return lax.psum(own, axis)
    k = 1
    while k < count:
        jumps = (k, 2 * k, 3 * k) if 4 * k <= count else (k,)
        own = own + sum(lax.ppermute(own, axis, [(i, i ^ j) for i in range(count)]) for j in jumps)
        k *= len(jumps) + 1
    return own


def halo(near, far, axis):
    count = lax.axis_size(axis)
    swap = lambda first: [p for i in range(first, count - 1, 2) for p in ((i, i + 1), (i + 1, i))]
    far = lax.ppermute(far, axis, swap(1))
    return lax.ppermute(near, axis, swap(0)), far


def body(
    latents,
    basis,
    conv_in,
    conv_mid,
    conv_out,
    pressure_prev,
    source,
    perf_cells,
    perf_count,
    obs_perturbed,
    obs_error,
):
    members = latents.shape[0]
    layers, rows, width = basis.shape[1:]
    tiles = lax.axis_size("tile")
    parts = lax.axis_size("mem")
    grid_rows = rows * tiles
    tile_vec = lax.axis_index("tile").astype(jnp.int32).reshape(1)
    mem_vec = lax.axis_index("mem").astype(jnp.int32).reshape(1)

    field, near, far = field_of(tile_vec, latents, basis, pressure_prev, source)
    near, far = halo(near, far, "tile")
    field, *weights = early(tile_vec, grid_rows, field, conv_in, conv_mid, conv_out.reshape(1, -1))
    *press, sums = decode(
        parts, tile_vec, mem_vec, grid_rows, field, near, far, pressure_prev, source,
        weights, perf_cells.T, perf_count.reshape(1, -1),
    )
    swaps = gathered(press, "mem")
    sums = summed(sums, "tile")
    well = jnp.concatenate([sums[:members] / sums[members:], latents], axis=1)
    pieces = gathered([well] * parts, "mem")
    press, data, new = update(mem_vec, pieces, swaps, obs_perturbed, obs_error.reshape(1, -1))
    return (press.reshape((parts * members,) + press.shape[2:]), data, new)


def solution(mesh):
    return jax.shard_map(
        body,
        mesh=mesh,
        in_specs=(
            P("mem", None),
            P(None, None, "tile", None),
            P(),
            P(),
            P(),
            P(None, "tile", None),
            P(None, "tile", None),
            P(),
            P(),
            P(),
            P(),
        ),
        out_specs=(P(None, None, "tile", "mem"), P(), P("mem", None)),
        check_vma=False,
    )
```

```python
import functools
import math

import jax
import jax.numpy as jnp
from jax import lax
from jax.experimental import pallas as pl
from jax.experimental.pallas import tpu as pltpu
from jax.sharding import PartitionSpec as P

SWEEPS = 2
PACKED = 80
HALO = 4
RING = 24
LIFT_BLOCKS = 11
INNER = (3, 8)
FIRST = ((4, 0), (5, 1), (6, 2))
ORDER = ((5, 7, 3), (6, 3, 4), (4, 8, 5), (7, 2, 1), (3, 9, 2), (8, 1, 0), (2, 10, 3), (9, 0, 4), (1, None, None), (10, None, None))
MIX_BLOCKS = 10
SEG = 16
BF = jnp.bfloat16
F32 = jnp.float32
VMEM = pl.BlockSpec(memory_space=pltpu.VMEM)
SMEM = pl.BlockSpec(memory_space=pltpu.SMEM)


def iota(shape, dim):
    return lax.broadcasted_iota(jnp.int32, shape, dim)


def place_weights(tile, grid_rows, rows, in_ref, mid_ref, out_ref, win_ref, wmix_ref, gain_ref):
    one = lambda mask: jnp.where(mask, 1.0, 0.0).astype(BF)
    dot = functools.partial(jnp.dot, preferred_element_type=F32)
    taps = dot(one(iota((64, 9), 0) & 15 == iota((64, 9), 1)), in_ref[...]).astype(BF)
    taps = dot(taps, one(iota((64, 256), 0) == iota((64, 256), 1) & 63))
    kinds = jnp.where(iota((64, 256), 0) >> 4 == iota((64, 256), 1) >> 6, taps, 0.0).astype(BF)
    k, j = iota((256, 64), 0), iota((256, 64), 1)
    lane = k & 127
    own = lane < 64
    offset = 2 * (k >> 7) + jnp.where(own, lane >> 5, ((lane - 64) >> 4) & 1)
    ring = jnp.where(own, lane & 15, jnp.where(lane < 96, 16 + (lane & 7), 2 * RING))
    place, tap = j >> 4, j & 15
    xx, yy = place >> 1, place & 1
    a = ((tap * 11) >> 5) - 1
    b = tap - 3 * (a + 1) - 1
    fits = (tap < 9) & (offset == yy + b + 1)
    for block in range(LIFT_BLOCKS):
        row = jnp.where(xx == 0, 18, -3) if block == 0 else 2 * block - HALO + xx
        near = row + a
        near = jnp.where(near < 0, near + RING, near)
        grid_row = tile * rows + row
        pick = fits & (ring == near) & (grid_row >= 0) & (grid_row < grid_rows)
        win_ref[block] = dot(one(pick), kinds).astype(BF)
    o, n = iota((64, 1024), 0), iota((64, 1024), 1)
    put = one(n & 255 == (o >> 5) * 128 + (n >> 8) * 32 + (o & 31))
    placed = [
        lax.dot_general(mid_ref[t], put, (((0,), (0,)), ((), ())), preferred_element_type=F32) for t in range(9)
    ]
    for kind in range(4):
        side, over = kind & 1, kind >> 1
        for place_in in range(4):
            xi, yi = place_in >> 1, place_in & 1
            total = jnp.zeros((64, 256), F32)
            for place_out in range(4):
                xo, yo = place_out >> 1, place_out & 1
                dx = xi - xo + (0 if not over else (2 if xi == 0 else -2))
                dy = yi - yo + (0 if not side else (2 if yi == 0 else -2))
                if abs(dx) <= 1 and abs(dy) <= 1:
                    t = 3 * (dx + 1) + dy + 1
                    total = total + placed[t][:, 256 * place_out : 256 * place_out + 256]
            at = 256 * kind + 64 * place_in
            wmix_ref[at : at + 64, :] = total.astype(BF)
    gains = jnp.broadcast_to(out_ref[...].astype(F32), (8, 64)).astype(BF)
    c, n = iota((64, 128), 0), iota((64, 128), 1)
    gain_ref[0:8] = dot(gains, one(c == n & 31))
    gain_ref[8:16] = dot(gains, one(c == 32 + (n & 31)))


def shifted(f):
    hi = f.astype(BF).astype(F32)
    lo = f - hi
    edge = iota(f.shape, 1) == 0
    return [jnp.where(edge, 0.0, pltpu.roll(v, 1, 1)) for v in (hi, lo)] + [hi, lo]


def turned(parts, span, scr):
    width = parts[0].shape[1]
    tall = jnp.concatenate(parts, axis=0).T
    scr[0:width, :] = tall
    end = pltpu.roll(tall[width - 8 : width], 128 - span // 2, 1)
    end = jnp.where(iota(end.shape, 1) & (span - 1) < span // 2, end, 0.0)
    scr[width : width + 8, :] = pltpu.roll(end, 1, 0)


def lift_block(pt, win, put_lift, put_side):
    total = pt.shape[0]
    wide = jnp.maximum(jnp.dot(pt, win, preferred_element_type=F32), 0.0)
    put_lift(wide.astype(BF))
    right = iota((SEG, 256), 1) & 64 == 0
    row = iota((SEG, 256), 0)
    steps = SEG
    for base in range(0, total, steps * SEG):
        last = base + (steps - 1) * SEG
        after = jnp.where(row < SEG - 1, pltpu.roll(wide[base : base + SEG], SEG - 1, 0), 0.0)
        before = jnp.where(row > 0, pltpu.roll(wide[last : last + SEG], 1, 0), 0.0)
        for q in range(steps):
            r = base + q * SEG
            nxt = after if q == steps - 1 else wide[r + SEG : r + 2 * SEG]
            prv = before if q == 0 else wide[r - SEG : r]
            put_side(r, jnp.where(right, nxt, prv).astype(BF))


def lift_to(pt_ref, win, lift_ref, side_ref, slot):
    def put_lift(v):
        lift_ref[slot] = v

    def put_side(r, v):
        side_ref[slot, r : r + SEG, :] = v

    lift_block(pt_ref[...], win, put_lift, put_side)


def early_kernel(field_ref, pt_ref, t_scr):
    layers, members, rows, width = field_ref.shape
    groups = layers * members
    steps = width // (2 * SEG)
    block_rows = width // 2

    def load(pair, _):
        parts = []
        for half in range(2):
            group = 2 * pair + half
            parts += shifted(field_ref[group // members, lax.rem(group, members)])
        turned(parts, 4 * rows, t_scr)
        mine = iota((SEG, 128), 1) < 4 * rows
        for q in range(steps + 1):
            part = t_scr[pl.ds(2 * q, SEG, stride=2 * steps), :]
            for half in range(2):
                v = jnp.where(mine, part if half == 0 else pltpu.roll(part, 64, 1), 0.0).astype(BF)
                at = (2 * pair + half) * block_rows + q * SEG
                if q < steps:
                    pt_ref[pl.ds(pl.multiple_of(at, SEG), SEG), 0:128] = v
                if q > 0:
                    pt_ref[pl.ds(pl.multiple_of(at - SEG, SEG), SEG), 128:256] = v
        return 0

    lax.fori_loop(0, groups // 2, load, 0)


def early(field):
    layers, members, rows, width = field.shape
    total = layers * members * width // 2
    return pl.pallas_call(
        early_kernel,
        in_specs=[VMEM],
        out_specs=VMEM,
        out_shape=jax.ShapeDtypeStruct((total, 256), BF),
        scratch_shapes=[pltpu.VMEM((width + 8, 128), F32)],
        compiler_params=pltpu.CompilerParams(vmem_limit_bytes=16 * 2**20),
        cost_estimate=pl.CostEstimate(flops=900_000_000, bytes_accessed=3_000_000, transcendentals=0),
    )(field)


def field_kernel(
    grid_rows,
    tile_ref,
    lat_hbm,
    basis_ref,
    prev_hbm,
    src_hbm,
    in_ref,
    mid_ref,
    out_ref,
    field_ref,
    near_ref,
    far_ref,
    win_ref,
    wmix_ref,
    gain_ref,
    held,
    lat_ref,
    prev_ref,
    src_ref,
    sems,
):
    chunks, comps, layers, rows, width = held.shape
    members, total = lat_ref.shape
    span = comps * rows
    copies = [
        pltpu.make_async_copy(basis_ref.at[pl.ds(c * comps, comps)], held.at[c], sems.at[c]) for c in range(chunks)
    ]
    small = [
        pltpu.make_async_copy(a, b, sems.at[chunks + i])
        for i, (a, b) in enumerate(((lat_hbm, lat_ref), (prev_hbm, prev_ref), (src_hbm, src_ref)))
    ]
    for copy in small[:1] + copies + small[1:]:
        copy.start()
    place_weights(tile_ref[0], grid_rows, rows, in_ref, mid_ref, out_ref, win_ref, wmix_ref, gain_ref)
    even_tile = tile_ref[0] & 1 == 0
    shape = (PACKED, 2 * (layers * members + 2 * layers) * rows)
    picks = [packed_from(layers, members, rows, up, shape) for up in (even_tile, jnp.logical_not(even_tile))]
    small[0].wait()
    lat = lat_ref[...].astype(BF)
    own = iota((rows, span), 0) == iota((rows, span), 1) & (rows - 1)
    behind = iota((total, span), 0) - split(iota((total, span), 1), rows)[0]
    for c in range(chunks):
        pick = jnp.where(behind == c * comps, 1.0, 0.0).astype(BF)
        spread = jnp.dot(lat, pick, preferred_element_type=F32)
        left = jnp.where(own[None], spread[:, None, :], 0.0).astype(BF).reshape(members * rows, span)
        copies[c].wait()
        for z in range(layers):
            part = jnp.dot(left, held[c, :, z].reshape(span, width), preferred_element_type=F32)
            part = part.reshape(members, rows, width)
            field_ref[z] = part if c == 0 else field_ref[z] + part
    small[1].wait()
    small[2].wait()
    exact, rest = [], []
    for value in (field_ref[...].reshape(-1, width), prev_ref[...].reshape(-1, width), src_ref[...].reshape(-1, width)):
        hi = value.astype(BF)
        exact.append(hi)
        rest.append((value - hi.astype(F32)).astype(BF))
    pool = jnp.concatenate([exact[0], rest[0], exact[1], rest[1], exact[2], rest[2]], axis=0)
    for ref, pick in zip((near_ref, far_ref), picks):
        ref[...] = jnp.dot(pick, pool, preferred_element_type=F32).astype(BF)


def packed_from(layers, members, rows, upper, shape):
    groups = layers * members
    r, at = iota((shape[0], 1), 0), iota(shape, 1)
    last = jnp.where(upper, 1, 0)
    group = (r * 52) >> 8
    j = r - 5 * group
    row_hi = jnp.where(last == 1, rows - HALO + j, j)
    row_lo = jnp.where(last == 1, rows - 1, 0)
    field = jnp.where(j < HALO, group * rows + row_hi, (groups + group) * rows + row_lo)
    p = r - 5 * groups
    half, j = (p >> 1) & 1, p & 1
    prev = (2 * groups + half * layers + (p >> 2)) * rows + jnp.where(last == 1, rows - 2 + j, j)
    s = p - 4 * layers
    src = (2 * groups + (2 + (s & 1)) * layers + (s >> 1)) * rows + jnp.where(last == 1, rows - 1, 0)
    wanted = jnp.where(p < 0, field, jnp.where(s < 0, prev, jnp.where(s < 2 * layers, src, -1)))
    return jnp.where(wanted == at, 1.0, 0.0).astype(BF)


def unpacked_to(layers, members, upper, shape):
    groups = layers * members
    r, at = iota((shape[0], 1), 0), iota(shape, 1)
    group, s = r >> 3, r & 7
    up = jnp.where(upper, 1, 0)
    j = jnp.where(up == 1, s - HALO, s)
    mine = (j >= 0) & (j < HALO)
    near = jnp.where(up == 1, j - 2, j)
    close = mine & (near >= 0) & (near < 2)
    z = group - groups
    hi = jnp.where(z < 0, group * 5 + j, 5 * groups + z * 4 + near)
    lo = jnp.where(z < 0, group * 5 + HALO, 5 * groups + z * 4 + 2 + near)
    is_src = z >= layers
    src = 5 * groups + 4 * layers + 2 * (z - layers)
    edge = close & (jnp.where(up == 1, near, 1 - near) == 1)
    hi = jnp.where(is_src, src, hi)
    lo = jnp.where(is_src, src + 1, lo)
    use_hi = (z < 0) & mine | (z >= 0) & (z < layers) & close | is_src & edge
    use_lo = (z >= 0) & (z < layers) & close | (z < 0) & edge | is_src & edge
    return jnp.where(use_hi & (at == hi) | use_lo & (at == lo), 1.0, 0.0).astype(BF)


def field_of(tile_vec, grid_rows, latents, basis, prev, src, conv_in, conv_mid, conv_out):
    total, layers, rows, width = basis.shape
    members = latents.shape[0]
    comps = 32
    return pl.pallas_call(
        functools.partial(field_kernel, grid_rows),
        in_specs=[SMEM] + [pl.BlockSpec(memory_space=pltpu.HBM)] * 4 + [VMEM] * 3,
        out_specs=[VMEM] * 6,
        out_shape=[
            pltpu.VMEM((layers, members, rows, width), F32),
            pltpu.VMEM((PACKED, width), BF),
            pltpu.VMEM((PACKED, width), BF),
            pltpu.VMEM((LIFT_BLOCKS, 256, 256), BF),
            pltpu.VMEM((1024, 256), BF),
            pltpu.VMEM((16, 128), F32),
        ],
        scratch_shapes=[
            pltpu.VMEM((total // comps, comps, layers, rows, width), BF),
            pltpu.VMEM(latents.shape, F32),
            pltpu.VMEM(prev.shape, F32),
            pltpu.VMEM(src.shape, F32),
            pltpu.SemaphoreType.DMA((total // comps + 3,)),
        ],
        compiler_params=pltpu.CompilerParams(vmem_limit_bytes=57 * 2**20),
    )(tile_vec, latents, basis, prev, src, conv_in, conv_mid, conv_out)


def target(me, k, count):
    return (me + k) % count if count & (count - 1) else me ^ k


def origin(me, k, count):
    return (me + count - k) % count if count & (count - 1) else me ^ k


def split(value, by):
    if by & (by - 1):
        return value // by, value % by
    return value >> (by.bit_length() - 1), value & (by - 1)


def decode_kernel(
    grid_rows,
    tile_ref,
    mem_ref,
    field_ref,
    near_ref,
    far_ref,
    prev_ref,
    src_ref,
    win_ref,
    wmix_ref,
    gain_ref,
    early_pt_ref,
    ids_ref,
    count_ref,
    *refs,

):
    parts = len(refs) - 11
    press_refs, sums_ref = refs[:parts], refs[parts]
    f_scr, t_scr, pt_scr, lift_scr, side_scr, deep_scr, wout_scr, v_scr, press_scr, third_scr = refs[parts + 1 :]
    layers, members, rows, width = field_ref.shape
    groups = layers * members
    steps = width // (2 * SEG)
    block_rows = width // 2
    tile, mem = tile_ref[0], mem_ref[0]
    even_tile = tile & 1 == 0

    shape = ((groups + 2 * layers) * 8, PACKED)
    from_near = unpacked_to(layers, members, jnp.logical_not(even_tile), shape)
    from_far = unpacked_to(layers, members, even_tile, shape)
    third_scr[...] = (
        jnp.dot(from_near, near_ref[...], preferred_element_type=F32)
        + jnp.dot(from_far, far_ref[...], preferred_element_type=F32)
    ).reshape(-1, 8, width)

    def load(quad):
        parts = []
        for j in range(4):
            parts += shifted(third_scr[4 * quad + j])
        turned(parts, 32, t_scr.at[quad])
        lane = iota((SEG, 128), 1)
        mine = (lane >= 64) & (lane < 96)
        for q in range(steps + 1):
            part = t_scr[quad, pl.ds(2 * q, SEG, stride=2 * steps), :]
            for j in range(4):
                v = part if j == 2 else pltpu.roll(part, (64 - 32 * j) % 128, 1)
                v = jnp.where(mine, v, 0.0).astype(BF)
                at = (4 * quad + j) * block_rows + q * SEG
                if q < steps:
                    rows_at = pl.ds(pl.multiple_of(at, SEG), SEG)
                    pt_scr[rows_at, 0:128] = early_pt_ref[rows_at, 0:128] + v
                if q > 0:
                    rows_at = pl.ds(pl.multiple_of(at - SEG, SEG), SEG)
                    pt_scr[rows_at, 128:256] = early_pt_ref[rows_at, 128:256] + v

    gain0, gain1 = gain_ref[0:1, :], gain_ref[8:9, :]

    places = {}

    begun = set()

    def mix(block, here, above, below):
        x = jnp.concatenate(
            [
                here[0][here[2]],
                here[1][here[2]],
                below[0][below[2], :, 0:128],
                above[0][above[2], :, 128:256],
                below[1][below[2], :, 0:128],
                above[1][above[2], :, 128:256],
            ],
            axis=1,
        )
        deep = jnp.maximum(jnp.dot(x, wmix_ref[...], preferred_element_type=F32), 0.0)
        deep = deep[:, :128] * gain0 + deep[:, 128:] * gain1
        place, part = divmod(block - 1, 4)
        deep = deep + pltpu.roll(deep, 16 if part & 2 else 112, 1)
        deep = deep + pltpu.roll(deep, 8 if part & 1 else 120, 1)
        deep = jnp.where((iota(deep.shape, 1) & 31) >> 3 == part, deep, 0.0).astype(BF)
        deep_scr[place] = deep if place not in begun else deep_scr[place] + deep
        begun.add(place)

    def lift(block, slot):
        lift_to(early_pt_ref if INNER[0] <= block <= INNER[1] else pt_scr, win_ref[block], lift_scr, side_scr, slot)
        places[block] = (lift_scr, side_scr, slot)

    for block, slot in FIRST:
        lift(block, slot)
    for step, (block, lifted, slot) in enumerate(ORDER):
        mix(block, places[block], places[block - 1], places[(block + 1) % LIFT_BLOCKS])
        if step < groups // 4:
            load(step)
        if lifted is not None:
            lift(lifted, slot)

    k, n = iota(wout_scr.shape, 0), iota(wout_scr.shape, 1)
    place = (k & 127) >> 5
    row = 2 * (4 * (k >> 7) + ((k & 31) >> 3) + 1) - HALO + (place >> 1)
    row = jnp.where(row < 0, row + RING, row)
    wout_scr[...] = jnp.where(n == (place & 1) * 32 + row, 1.0, 0.0).astype(BF)

    def collect(pair, held):
        at = pl.ds(pl.multiple_of(pair * 2 * block_rows, 2 * block_rows), 2 * block_rows)
        x = jnp.concatenate([deep_scr[j, at, :] for j in range(deep_scr.shape[0])], axis=1)
        both = jnp.dot(x, wout_scr[...], preferred_element_type=F32)
        both = both[:block_rows] + pltpu.roll(both[block_rows:], 64, 1)
        for q in range(steps):
            part = both[q * SEG : (q + 1) * SEG]
            t_scr[held, pl.ds(2 * q, SEG, stride=2 * steps), :] = part
            t_scr[held, pl.ds(2 * q + 1, SEG, stride=2 * steps), :] = part
        flat = t_scr[held, 0:width, :].T
        even = iota((RING, width), 1) & 1 == 0
        for half in range(2):
            s = 64 * half
            group = 2 * pair + half
            f = jnp.concatenate([field_ref[group // members, group % members], third_scr[group]], axis=0)
            f_scr[group] = f + jnp.where(
                even, flat[s : s + RING], flat[s + 32 : s + 32 + RING]
            )

    for pair in range(groups // 2):
        collect(pair, pair % (groups // 4))

    full = (RING, width)
    ring = iota(full, 0)
    grid_row = tile * rows + jnp.where(ring < rows + HALO, ring, ring - RING)
    inside = (grid_row >= 0) & (grid_row < grid_rows)
    joined = (grid_row >= 0) & (grid_row < grid_rows - 1)
    not_last = iota(full, 1) < width - 1

    def ring_of(ref, group, z):
        return jnp.concatenate([ref[z], third_scr[group]], axis=0)

    def row_next(v):
        return pltpu.roll(v, RING - 1, 0)

    def row_prev(v):
        return pltpu.roll(v, 1, 0)

    def col_next(v):
        return pltpu.roll(v, width - 1, 1)

    def col_prev(v):
        return pltpu.roll(v, 1, 1)

    start = [ring_of(prev_ref, groups + z, z) for z in range(layers)]
    base = [start[z] + ring_of(src_ref, groups + layers + z, z) for z in range(layers)]
    around = [[f(start[z]) for f in (row_next, row_prev, col_next, col_prev)] for z in range(layers)]

    def flow(p, q):
        return 2.0 * p * q / (p + q)

    def sweep(member, _):
        perm = [jnp.where(inside, jnp.exp(f_scr[z * members + member]), 1.0) for z in range(layers)]
        between = jnp.where(inside, flow(perm[0], perm[1]), 0.0)
        faces, scale = [], []
        for z in range(layers):
            below = jnp.where(joined, flow(perm[z], row_next(perm[z])), 0.0)
            right = jnp.where(not_last, flow(perm[z], col_next(perm[z])), 0.0)
            right = jnp.where(inside, right, 0.0)
            face = (below, row_prev(below), right, col_prev(right))
            faces.append(face)
            scale.append(1.0 / (1.0 + between + face[0] + face[1] + face[2] + face[3]))
        press, near = start, around
        for turn in range(SWEEPS):
            if turn > 0:
                near = [[f(press[z]) for f in (row_next, row_prev, col_next, col_prev)] for z in range(layers)]
            press = [
                (base[z] + between * press[1 - z] + sum(c * v for c, v in zip(faces[z], near[z]))) * scale[z]
                for z in range(layers)
            ]
        cols = width // parts
        for z in range(layers):
            press_scr[...] = press[z][:rows]
            for k in range(parts):
                at = pl.multiple_of(target(mem, k, parts) * cols, cols)
                press_refs[k][member, z] = press_scr[:, pl.ds(at, cols)]
            weight = perm[z][:rows]
            for kind, value in enumerate((weight * press[z][:rows], weight)):
                hi = value.astype(BF)
                lo = (value - hi.astype(F32)).astype(BF)
                for part, piece in enumerate((hi, lo)):
                    at = (((kind * 2 + part) * members + member) * layers + z) * rows
                    v_scr[pl.ds(pl.multiple_of(at, rows), rows), :] = piece
        return 0

    lax.fori_loop(0, members, sweep, 0)

    slots, wells = ids_ref.shape
    cells = layers * rows
    layer_at, rest = split(ids_ref[...], grid_rows * width)
    row_at, col = split(rest, width)
    row_at = row_at - tile * rows
    used = (iota((slots, wells), 0) < count_ref[...]) & (row_at >= 0) & (row_at < rows)
    sel = jnp.where(used, layer_at * rows + row_at, -1)
    sums = jnp.zeros((4 * members, wells), F32)
    for slot in range(0, slots, 2):
        sel_two = jnp.concatenate([sel[slot : slot + 1], sel[slot + 1 : slot + 2]], axis=1)
        col_two = jnp.concatenate([col[slot : slot + 1], col[slot + 1 : slot + 2]], axis=1)
        here = iota((width, 2 * wells), 0) == col_two
        got = jnp.dot(v_scr[...], jnp.where(here, 1.0, 0.0).astype(BF), preferred_element_type=F32)
        mine = iota((cells, 2 * wells), 0) == sel_two
        picked = jnp.where(mine[None], got.reshape(4 * members, cells, 2 * wells), 0.0)
        both = jnp.sum(picked, axis=1)
        sums = sums + both[:, :wells] + both[:, wells:]
    sums_ref[0:members] = sums[0:members] + sums[members : 2 * members]
    sums_ref[members : 2 * members] = sums[2 * members : 3 * members] + sums[3 * members :]


def decode(parts, tile_vec, mem_vec, grid_rows, field, near, far, prev, src, weights, ids, counts):
    layers, members, rows, width = field.shape
    groups = layers * members
    total = groups * width // 2
    wells = ids.shape[1]
    return pl.pallas_call(
        functools.partial(decode_kernel, grid_rows),
        in_specs=[SMEM] * 2 + [VMEM] * 11,
        out_specs=[VMEM] * (parts + 1),
        out_shape=[jax.ShapeDtypeStruct((members, layers, rows, width // parts), F32)] * parts
        + [jax.ShapeDtypeStruct((2 * members, wells), F32)],
        scratch_shapes=[
            pltpu.VMEM((groups, RING, width), F32),
            pltpu.VMEM((groups // 4, width + 8, 128), F32),
            pltpu.VMEM((total, 256), BF),
            pltpu.VMEM((1 + max(o[2] for o in ORDER if o[2] is not None), total, 256), BF),
            pltpu.VMEM((1 + max(o[2] for o in ORDER if o[2] is not None), total, 256), BF),
            pltpu.VMEM((-(-MIX_BLOCKS // 4), total, 128), BF),
            pltpu.VMEM((-(-MIX_BLOCKS // 4) * 128, 128), BF),
            pltpu.VMEM((4 * groups * rows, width), BF),
            pltpu.VMEM((rows, width), F32),
            pltpu.VMEM((groups + 2 * layers, 8, width), F32),
        ],
        compiler_params=pltpu.CompilerParams(vmem_limit_bytes=43 * 2**20),
    )(tile_vec, mem_vec, field, near, far, prev, src, *weights, ids, counts)


def update_kernel(mem_ref, refs, swap_refs, obs_ref, err_ref, press_ref, data_ref, new_ref, all_scr, step_scr):
    count = len(refs)
    own = refs[0].shape[0]
    members, wells = obs_ref.shape
    mem = mem_ref[0]
    for k in range(count):
        source = origin(mem, k, count)
        all_scr[source] = refs[k][...]
        press_ref[source] = swap_refs[k][...]
    every = jnp.concatenate([all_scr[k] for k in range(count)], axis=0)
    data, every = every[:, :wells], every[:, wells:]
    data_ref[...] = data
    scale = 2.0 * err_ref[...]
    root = math.sqrt(members - 1)
    scaled = (data - jnp.mean(data, axis=0, keepdims=True)) / (root * scale)
    innov = (obs_ref[...] - data) / scale
    dims = (((1,), (1,)), ((), ()))
    exact = lax.Precision.HIGHEST
    eye = (iota((members, members), 0) == iota((members, members), 1)).astype(F32)
    gram = eye + lax.dot_general(scaled, scaled, dims, precision=exact, preferred_element_type=F32)
    cross = lax.dot_general(innov, scaled, dims, precision=exact, preferred_element_type=F32)
    right = (every - jnp.mean(every, axis=0, keepdims=True)) / root
    place = iota((members, 128), 0)
    places = iota(right.shape, 0)
    cols = [jnp.broadcast_to(gram[:, k : k + 1], (members, 128)) for k in range(members)]
    for k in range(members):
        inverse = 1.0 / cols[k][k : k + 1]
        factor = jnp.where(place == k, 0.0, cols[k])
        for i in range(k + 1, members):
            row = cols[i][k : k + 1] * inverse
            cols[i] = jnp.where(place == k, row, cols[i] - factor * row)
        row = right[k : k + 1] * jnp.concatenate([inverse] * (right.shape[1] // 128), axis=1)
        wide = jnp.concatenate([factor] * (right.shape[1] // 128), axis=1)
        right = jnp.where(places == k, row, right - wide * row)
    new = every + jnp.dot(cross, right, precision=exact, preferred_element_type=F32)
    for k in range(count):
        step_scr[k] = new[k * own : (k + 1) * own]
    new_ref[...] = step_scr[mem]


def update(mem_vec, pieces, swaps, obs, err):
    count = len(pieces)
    own, total = pieces[0].shape
    members, wells = obs.shape

    def kernel(mem_ref, *refs):
        update_kernel(mem_ref, refs[:count], refs[count : 2 * count], *refs[2 * count :])

    return pl.pallas_call(
        kernel,
        in_specs=[SMEM] + [VMEM] * (2 * count + 2),
        out_specs=[VMEM] * 3,
        out_shape=[
            jax.ShapeDtypeStruct((count,) + swaps[0].shape, F32),
            jax.ShapeDtypeStruct((members, wells), F32),
            jax.ShapeDtypeStruct((own, total - wells), F32),
        ],
        scratch_shapes=[
            pltpu.VMEM((count, own, total), F32),
            pltpu.VMEM((count, own, total - wells), F32),
        ],
        compiler_params=pltpu.CompilerParams(vmem_limit_bytes=24 * 2**20),
    )(mem_vec, *pieces, *swaps, obs, err)


def gathered(pieces, axis):
    count = lax.axis_size(axis)
    return [pieces[0]] + [
        lax.ppermute(pieces[k], axis, [(i, target(i, k, count)) for i in range(count)]) for k in range(1, count)
    ]


def summed(own, axis):
    count = lax.axis_size(axis)
    if count & (count - 1):
        return lax.psum(own, axis)
    k = 1
    while k < count:
        jumps = (k, 2 * k, 3 * k) if 4 * k <= count else (k,)
        own = own + sum(lax.ppermute(own, axis, [(i, i ^ j) for i in range(count)]) for j in jumps)
        k *= len(jumps) + 1
    return own


def halo(near, far, axis):
    count = lax.axis_size(axis)
    swap = lambda first: [p for i in range(first, count - 1, 2) for p in ((i, i + 1), (i + 1, i))]
    far = lax.ppermute(far, axis, swap(1))
    return lax.ppermute(near, axis, swap(0)), far


def body(
    latents,
    basis,
    conv_in,
    conv_mid,
    conv_out,
    pressure_prev,
    source,
    perf_cells,
    perf_count,
    obs_perturbed,
    obs_error,
):
    members = latents.shape[0]
    layers, rows, width = basis.shape[1:]
    tiles = lax.axis_size("tile")
    parts = lax.axis_size("mem")
    grid_rows = rows * tiles
    tile_vec = lax.axis_index("tile").astype(jnp.int32).reshape(1)
    mem_vec = lax.axis_index("mem").astype(jnp.int32).reshape(1)

    field, near, far, *weights = field_of(
        tile_vec, grid_rows, latents, basis, pressure_prev, source, conv_in, conv_mid, conv_out.reshape(1, -1)
    )
    near, far = halo(near, far, "tile")
    weights.append(early(field))
    *press, sums = decode(
        parts, tile_vec, mem_vec, grid_rows, field, near, far, pressure_prev, source,
        weights, perf_cells.T, perf_count.reshape(1, -1),
    )
    swaps = gathered(press, "mem")
    sums = summed(sums, "tile")
    well = jnp.concatenate([sums[:members] / sums[members:], latents], axis=1)
    pieces = gathered([well] * parts, "mem")
    press, data, new = update(mem_vec, pieces, swaps, obs_perturbed, obs_error.reshape(1, -1))
    return (press.reshape((parts * members,) + press.shape[2:]), data, new)


def solution(mesh):
    return jax.shard_map(
        body,
        mesh=mesh,
        in_specs=(
            P("mem", None),
            P(None, None, "tile", None),
            P(),
            P(),
            P(),
            P(None, "tile", None),
            P(None, "tile", None),
            P(),
            P(),
            P(),
            P(),
        ),
        out_specs=(P(None, None, "tile", "mem"), P(), P("mem", None)),
        check_vma=False,
    )
```
